32 devices in a mesh: ctx: 8 (over z, x), tp: 4 (over y, core).
Axes of the slice: x: 2, y: 2, z: 4, core: 2. Of those that a mesh axis runs over, the one named last changes fastest.
Arguments:
- tokens: bfloat16 [2, 4096, 2048], P(None, 'ctx', 'tp'), may hold values from -6 to 6
- lengths: int32 [2], replicated, may hold values from 256 to 4096, as said below
- teacher: bfloat16 [2, 4096, 2048], P(None, 'ctx', 'tp'), may hold values from -6 to 6
- out_grad: bfloat16 [2, 4096, 2048], P(None, 'ctx', 'tp'), may hold values from -6 to 6
- w_query: bfloat16 [2048, 2048], P(None, 'tp'), may hold values from -0.125 to 0.125
- b_query: bfloat16 [2048], P('tp'), may hold values from -3 to 3
- w_keyval: bfloat16 [2048, 256], replicated, may hold values from -0.125 to 0.125
- b_value: bfloat16 [128], replicated, may hold values from -0.29882812 to 0.29882812
- w_output: bfloat16 [2048, 2048], P('tp'), may hold values from -1 to 1
- b_output: bfloat16 [2048], P('tp'), may hold values from -0.29882812 to 0.29882812
- w_expand: bfloat16 [2048, 8192], P(None, 'tp'), may hold values from -0.125 to 0.125
- b_expand: bfloat16 [8192], P('tp'), may hold values from -0.29882812 to 0.29882812
- w_shrink: bfloat16 [8192, 2048], P('tp'), may hold values from -0.0625 to 0.0625
- b_shrink: bfloat16 [2048], P('tp'), may hold values from -0.29882812 to 0.29882812
- gain_first: bfloat16 [2048], P('tp'), may hold values from 0.099609375 to 1.8984375
- bias_first: bfloat16 [2048], P('tp'), may hold values from -0.1796875 to 0.1796875
- gain_second: bfloat16 [2048], P('tp'), may hold values from 0.099609375 to 1.8984375
- bias_second: bfloat16 [2048], P('tp'), may hold values from -0.1796875 to 0.1796875
Outputs:
- output: bfloat16 [2, 4096, 2048], P(None, 'ctx', 'tp')
- tokens_grad: float32 [2, 4096, 2048], P(None, 'ctx', 'tp')
- loss: float32 [], replicated
- grad_w_query: float32 [2048, 2048], P(None, 'tp')
- grad_b_query: float32 [2048], P('tp')
- grad_w_keyval: float32 [2048, 256], replicated
- grad_b_value: float32 [128], replicated
- grad_w_output: float32 [2048, 2048], P('tp')
- grad_b_output: float32 [2048], P('tp')
- grad_w_expand: float32 [2048, 8192], P(None, 'tp')
- grad_b_expand: float32 [8192], P('tp')
- grad_w_shrink: float32 [8192, 2048], P('tp')
- grad_b_shrink: float32 [2048], P('tp')
- grad_gain_first: float32 [2048], P('tp')
- grad_bias_first: float32 [2048], P('tp')
- grad_gain_second: float32 [2048], P('tp')
- grad_bias_second: float32 [2048], P('tp')
The draws below stay inside these ranges and needn't reach their ends.
Inputs may be any that keep to these rules, and one draw needn't show every extreme that they name: `lengths`: each sequence's valid tokens form a prefix; in every draw one sequence, drawn from the seed, is valid in full.
All inputs are finite; a program needn't handle non-finite values.
Results may differ from the reference program's by a relative error of at most 0.015.
Values may be sent and summed in bfloat16 or wider, within the bound.
No kernel may reach another device: no remote copies, remote signals or barrier semaphores. Data moves between devices by JAX's collectives and lax.ppermute only.
A program may use at most 256 MiB of HBM per device.

```python
import math
import jax
import jax.numpy as jnp
from jax import lax

D = 2048
H = 16
HD = 128
FF = 8192
SEQS = 2
BLOCK = 256
SEQ_LEN = 4096


def draw_lengths(key, part):
    key = jax.random.fold_in(key, 7)
    first, second = jax.random.split(key)
    counts = jax.random.randint(first, (SEQS,), BLOCK, SEQ_LEN + 1)
    whole = jax.random.randint(second, (), 0, SEQS)
    return jnp.where(jnp.arange(SEQS) == whole, SEQ_LEN, counts).astype(jnp.int32)


def steps_of(key, dims, pieces, least, top_value):
    level, own = 1.0, jax.random.fold_in(key, 6)
    for dim, shards_of in pieces:
        draws = jnp.exp(jax.random.uniform(jax.random.fold_in(own, dim), (shards_of,), jnp.float32, least / len(pieces), top_value / len(pieces)))
        level = level * jnp.repeat(draws, dims[dim] // shards_of).reshape([-1 if axis == dim else 1 for axis in range(len(dims))])
    return level


def noise(rng, shape, width, reach, cuts=(), held_as=jnp.bfloat16):
    loudness = steps_of(rng, shape, cuts, -0.22, 0.18) if cuts else 1.0
    values = jax.random.normal(rng, shape, jnp.float32) * width * loudness
    return jnp.minimum(jnp.maximum(values, -reach), reach).astype(held_as)


def setup_inputs(seed: int = 0) -> dict:
    seeds = jax.random.split(jax.random.key(seed), 19)
    tokens = noise(seeds[0], (SEQS, SEQ_LEN, D), 1.0, 6.0, ((1, 8), (2, 4)))
    lengths = draw_lengths(jax.random.fold_in(seeds[18], 71), 0)
    teacher = noise(seeds[2], (SEQS, SEQ_LEN, D), 1.0, 6.0, ((1, 8), (2, 4)))
    out_grad = noise(seeds[3], (SEQS, SEQ_LEN, D), 1.0, 6.0, ((1, 8), (2, 4)))
    w_query = noise(seeds[4], (D, H * HD), D ** -0.5, 0.125, ((1, 4),))
    b_query = noise(seeds[5], (H * HD,), 0.5, 3.0, ((0, 4),))
    w_keyval = noise(seeds[6], (D, 2 * HD), D ** -0.5, 0.125)
    b_value = noise(seeds[7], (HD,), 0.05, 0.29882812)
    w_output = noise(seeds[8], (H * HD, D), (H * HD // 64) ** -0.5, 1.0, ((0, 4),))
    b_output = noise(seeds[9], (D,), 0.05, 0.29882812, ((0, 4),))
    w_expand = noise(seeds[10], (D, FF), D ** -0.5, 0.125, ((1, 4),))
    b_expand = noise(seeds[11], (FF,), 0.05, 0.29882812, ((0, 4),))
    w_shrink = noise(seeds[12], (FF, D), FF ** -0.5, 0.0625, ((0, 4),))
    b_shrink = noise(seeds[13], (D,), 0.05, 0.29882812, ((0, 4),))
    gain_first = jnp.clip(1.0 + 0.18 * jax.random.normal(seeds[14], (D,), jnp.float32), 0.099609375, 1.8984375).astype(jnp.bfloat16)
    bias_first = noise(seeds[15], (D,), 0.03, 0.1796875, ((0, 4),))
    gain_second = jnp.clip(1.0 + 0.18 * jax.random.normal(seeds[16], (D,), jnp.float32), 0.099609375, 1.8984375).astype(jnp.bfloat16)
    bias_second = noise(seeds[17], (D,), 0.03, 0.1796875, ((0, 4),))
    return {"tokens": tokens, "lengths": lengths, "teacher": teacher, "out_grad": out_grad, "w_query": w_query, "b_query": b_query, "w_keyval": w_keyval, "b_value": b_value, "w_output": w_output, "b_output": b_output, "w_expand": w_expand, "b_expand": b_expand, "w_shrink": w_shrink, "b_shrink": b_shrink, "gain_first": gain_first, "bias_first": bias_first, "gain_second": gain_second, "bias_second": bias_second}


@jax.custom_vjp
def low(v):
    return lax.optimization_barrier(v.astype(jnp.bfloat16)).astype(jnp.float32)

@jax.custom_vjp
def low_back(v):
    return v

def low_keep(v):
    return (low(v), None)

def low_pass(kept, grad):
    return (grad,)

def back_keep(v):
    return (v, None)

def back_low(kept, grad):
    return (low(grad),)
low.defvjp(low_keep, low_pass)
low_back.defvjp(back_keep, back_low)
HIGH = lax.Precision.HIGHEST
EPS = 1e-05
NEG = -1e+30

def matmul(left, right):
    return jnp.dot(left, right, precision=HIGH)

def gelu_tanh(values):
    return jax.nn.gelu(values, approximate=True)

def layer_norm(values, gain, shift):
    mean = lax.optimization_barrier(jnp.mean(values, axis=-1, keepdims=True))
    centered = values - mean
    var = lax.optimization_barrier(jnp.mean(centered * centered, axis=-1, keepdims=True))
    return centered * lax.rsqrt(var + EPS) * gain + shift

def attend(queries, keys, values, count):
    heads = queries.reshape(SEQ_LEN, H, HD)
    key_pos = jnp.arange(SEQ_LEN).astype(jnp.int32)
    rows_each = math.gcd(SEQ_LEN, 512)

    def one_block(start):
        block_q = lax.dynamic_slice_in_dim(heads, start, rows_each, 0)
        query_pos = start + jnp.arange(rows_each).astype(jnp.int32)
        allowed = ((key_pos // BLOCK)[None, :] <= (query_pos // BLOCK)[:, None]) & (key_pos < count)[None, :]
        raw = low_back(jnp.einsum('qhd,kd->qhk', block_q, keys, precision=HIGH) * HD ** (-0.5))
        scores = jnp.where(allowed[:, None, :], raw, NEG)
        top = lax.optimization_barrier(jnp.max(scores, axis=-1, keepdims=True))
        expo = jnp.exp(scores - top)
        weights = low(expo / lax.optimization_barrier(jnp.sum(expo, axis=-1, keepdims=True)))
        return jnp.einsum('qhk,kd->qhd', weights, values, precision=HIGH)
    starts = (jnp.arange(SEQ_LEN // rows_each) * rows_each).astype(jnp.int32)
    mixed = lax.map(jax.checkpoint(one_block), starts)
    return mixed.reshape(SEQ_LEN, H * HD)

def layer(inputs, count, target, weight_out, params):
    w_query, b_query, w_keyval, b_value, w_output, b_output, w_expand, b_expand, w_shrink, b_shrink, gain_first, bias_first, gain_second, bias_second = params
    first = low(layer_norm(inputs, gain_first, bias_first))
    queries = low(low_back(matmul(first, w_query) + b_query))
    kv_bias = jnp.concatenate([jnp.zeros((HD,), jnp.float32), b_value])
    keyval = low(low_back(matmul(first, w_keyval) + kv_bias))
    mixed = attend(queries, keyval[:, :HD], keyval[:, HD:], count)
    attended = low(low_back(mixed))
    middle = inputs + low_back(matmul(attended, w_output) + b_output)
    second = low(layer_norm(middle, gain_second, bias_second))
    hidden = low_back(matmul(second, w_expand) + b_expand)
    activated = low(gelu_tanh(hidden))
    final = middle + low_back(matmul(activated, w_shrink) + b_shrink)
    valid = (jnp.arange(SEQ_LEN).astype(jnp.int32) < count).astype(jnp.float32)[:, None]
    diff = final - target
    part = jnp.sum(valid * (weight_out * final + 0.5 * diff * diff))
    return (final, part)

def reference(tokens, lengths, teacher, out_grad, w_query, b_query, w_keyval, b_value, w_output, b_output, w_expand, b_expand, w_shrink, b_shrink, gain_first, bias_first, gain_second, bias_second):
    params = tuple((p.astype(jnp.float32) for p in (w_query, b_query, w_keyval, b_value, w_output, b_output, w_expand, b_expand, w_shrink, b_shrink, gain_first, bias_first, gain_second, bias_second)))
    inputs = tokens.astype(jnp.float32)
    target = teacher.astype(jnp.float32)
    weight_out = out_grad.astype(jnp.float32)

    def objective(values, weights):
        total = jnp.zeros((), jnp.float32)
        finals = []
        for seq in range(SEQS):
            final, part = layer(values[seq], lengths[seq], target[seq], weight_out[seq], weights)
            finals.append(final)
            total = total + part
        return (total, jnp.stack(finals))
    total, pull, finals = jax.vjp(objective, inputs, params, has_aux=True)
    tokens_grad, grads = pull(jnp.ones((), jnp.float32))
    loss = total / (jnp.sum(lengths).astype(jnp.float32) * D)
    return (finals.astype(jnp.bfloat16), tokens_grad, loss, grads[0], grads[1], grads[2], grads[3], grads[4], grads[5], grads[6], grads[7], grads[8], grads[9], grads[10], grads[11], grads[12], grads[13])
```

```python
import functools
import math

import jax
import jax.numpy as jnp
from jax import lax
from jax.experimental import pallas as pl
from jax.experimental.pallas import tpu as pltpu
from jax.sharding import PartitionSpec as P

BLOCK = 256
EPS = 1e-05
NEG = -1e30
LOG2E = math.log2(math.e)
CORES = 2
MIB = 2**20
F32 = jnp.float32
BF16 = jnp.bfloat16


def dot_nn(left, right):
    return lax.dot_general(left, right, (((1,), (0,)), ((), ())), preferred_element_type=F32)


def dot_nt(left, right):
    return lax.dot_general(left, right, (((1,), (1,)), ((), ())), preferred_element_type=F32)


def dot_tn(left, right):
    return lax.dot_general(left, right, (((0,), (0,)), ((), ())), preferred_element_type=F32)


def attend_kernel(heads, head, rows, per, info, q_ref, kv_ref, mix_ref, att_ref, lse_ref, acc, top):
    block = pl.program_id(0)
    length, position = info[0], info[1]
    scale = head**-0.5 * LOG2E
    keys = jnp.minimum((position * pl.num_programs(0) + block + 1) * BLOCK, length)
    chunk = per * rows
    acc[...] = jnp.zeros_like(acc)
    top[...] = jnp.full_like(top, NEG)

    def step(index, masked):
        start = index * chunk
        spots = [pl.multiple_of(info[2 + index * per + i] * rows, rows) for i in range(per)]
        k = jnp.concatenate([kv_ref[pl.ds(spot, rows), :head] for spot in spots], axis=0)
        v = jnp.concatenate([kv_ref[pl.ds(spot, rows), head:] for spot in spots], axis=0)
        wide = jnp.concatenate([v, jnp.ones_like(v)], axis=1)
        for h in range(heads):
            s = dot_nt(q_ref[:, h * head : (h + 1) * head], k) * scale
            if masked:
                col = start + lax.broadcasted_iota(jnp.int32, s.shape, 1)
                s = jnp.where(col < keys, s, NEG)
            old = top[h]
            new = jnp.maximum(old, jnp.max(s, axis=1, keepdims=True))
            p = jnp.exp2(s - new[:, :1])
            top[h] = new
            acc[h] = acc[h] * jnp.exp2(old - new)[:, :1] + dot_nn(p.astype(BF16), wide)

    def body(index, carry):
        step(index, False)
        return carry

    whole = keys // chunk
    lax.fori_loop(0, whole, body, 0)

    @pl.when(keys % chunk != 0)
    def _():
        step(whole, True)

    for h in range(heads):
        cols = slice(h * head, (h + 1) * head)
        total = acc[h][:, head:]
        mixed = acc[h][:, :head] / total
        mix_ref[:, cols] = mixed
        att_ref[:, cols] = mixed.astype(BF16)
        lse_ref[:, cols] = top[h] + jnp.log2(total)


def attend(q, kv, info, head):
    rows, width = q.shape
    full = kv.shape[0]
    heads = width // head
    per = math.gcd(full // rows, max(1, 1024 // rows))
    block = pl.BlockSpec((BLOCK, width), lambda i, info: (i, 0))
    pairs = rows * heads * full
    return pl.pallas_call(
        functools.partial(attend_kernel, heads, head, rows, per),
        grid_spec=pltpu.PrefetchScalarGridSpec(
            num_scalar_prefetch=1,
            grid=(rows // BLOCK,),
            in_specs=[block, pl.BlockSpec((full, 2 * head), lambda i, info: (0, 0))],
            out_specs=[block, block, block],
            scratch_shapes=[
                pltpu.VMEM((heads, BLOCK, 2 * head), F32),
                pltpu.VMEM((heads, BLOCK, head), F32),
            ],
        ),
        out_shape=[
            jax.ShapeDtypeStruct((rows, width), F32),
            jax.ShapeDtypeStruct((rows, width), BF16),
            jax.ShapeDtypeStruct((rows, width), F32),
        ],
        compiler_params=pltpu.CompilerParams(vmem_limit_bytes=40 * MIB),
        cost_estimate=pl.CostEstimate(
            flops=8 * pairs * head, bytes_accessed=4 * MIB, transcendentals=pairs
        ),
    )(info, q, kv)


def attend_back_kernel(
    heads, head, rows, per, info, q_ref, do_ref, mix_ref, lse_ref, kv_ref, dq_ref, dkv_ref, dkv, dq, dlt
):
    block = pl.program_id(0)
    length, position = info[0], info[1]
    blocks = pl.num_programs(0)
    factor = head**-0.5
    scale = factor * LOG2E
    chunk = per * rows
    first = (position * blocks + block) * BLOCK
    keys = jnp.where(first < length, jnp.minimum(first + BLOCK, length), 0)

    @pl.when(block == 0)
    def _():
        dkv[...] = jnp.zeros_like(dkv)

    dq[...] = jnp.zeros_like(dq)
    for h in range(heads):
        cols = slice(h * head, (h + 1) * head)
        delta = jnp.sum(do_ref[:, cols].astype(F32) * mix_ref[:, cols], axis=1, keepdims=True)
        dlt[h] = jnp.broadcast_to(delta, (BLOCK, head))

    def step(index, masked):
        start = index * chunk
        spots = [pl.multiple_of(info[2 + index * per + i] * rows, rows) for i in range(per)]
        k = jnp.concatenate([kv_ref[pl.ds(spot, rows), :head] for spot in spots], axis=0)
        v = jnp.concatenate([kv_ref[pl.ds(spot, rows), head:] for spot in spots], axis=0)
        dk_sum = dv_sum = None
        for h in range(heads):
            cols = slice(h * head, (h + 1) * head)
            q, do = q_ref[:, cols], do_ref[:, cols]
            p = jnp.exp2(dot_nt(q, k) * scale - lse_ref[:, h * head : h * head + 1])
            if masked:
                col = start + lax.broadcasted_iota(jnp.int32, p.shape, 1)
                p = jnp.where(col < keys, p, 0.0)
            ds = (p * (dot_nt(do, v) - dlt[h][:, :1])).astype(BF16)
            dq[h] += dot_nn(ds, k)
            dk, dv = dot_tn(ds, q), dot_tn(p.astype(BF16), do)
            dk_sum, dv_sum = (dk, dv) if h == 0 else (dk_sum + dk, dv_sum + dv)
        for i, spot in enumerate(spots):
            part = slice(i * rows, (i + 1) * rows)
            dkv[pl.ds(spot, rows), :head] += dk_sum[part]
            dkv[pl.ds(spot, rows), head:] += dv_sum[part]

    def body(index, carry):
        step(index, False)
        return carry

    whole = keys // chunk
    lax.fori_loop(0, whole, body, 0)

    @pl.when(keys % chunk != 0)
    def _():
        step(whole, True)

    for h in range(heads):
        dq_ref[:, h * head : (h + 1) * head] = (dq[h] * factor).astype(BF16)

    @pl.when(block == blocks - 1)
    def _():
        dkv_ref[:, :head] = (dkv[:, :head] * factor).astype(BF16)
        dkv_ref[:, head:] = dkv[:, head:].astype(BF16)


def attend_back(q, do, mixed, lse, kv, info, head):
    rows, width = q.shape
    full = kv.shape[0]
    heads = width // head
    per = math.gcd(full // rows, max(1, 1024 // rows))
    block = pl.BlockSpec((BLOCK, width), lambda i, info: (i, 0))
    whole = pl.BlockSpec((full, 2 * head), lambda i, info: (0, 0))
    pairs = rows * heads * full
    return pl.pallas_call(
        functools.partial(attend_back_kernel, heads, head, rows, per),
        grid_spec=pltpu.PrefetchScalarGridSpec(
            num_scalar_prefetch=1,
            grid=(rows // BLOCK,),
            in_specs=[block, block, block, block, whole],
            out_specs=[block, whole],
            scratch_shapes=[
                pltpu.VMEM((full, 2 * head), F32),
                pltpu.VMEM((heads, BLOCK, head), F32),
                pltpu.VMEM((heads, BLOCK, head), F32),
            ],
        ),
        out_shape=[
            jax.ShapeDtypeStruct((rows, width), BF16),
            jax.ShapeDtypeStruct((full, 2 * head), BF16),
        ],
        compiler_params=pltpu.CompilerParams(vmem_limit_bytes=56 * MIB),
        cost_estimate=pl.CostEstimate(
            flops=12 * pairs * head, bytes_accessed=8 * MIB, transcendentals=pairs
        ),
    )(info, q, do, mixed, lse, kv)


def grad_kernel(count, *refs):
    total = dot_tn(refs[0][...], refs[count][...])
    for i in range(1, count):
        total += dot_tn(refs[i][...], refs[count + i][...])
    refs[-1][...] = total.astype(BF16)


def weight_grad(lefts, rights):
    rows, m = lefts[0].shape
    n = rights[0].shape[1]
    bm = min(m, 256)
    count = len(lefts)
    return pl.pallas_call(
        functools.partial(grad_kernel, count),
        grid=(m // bm,),
        in_specs=[pl.BlockSpec((rows, bm), lambda i: (0, i))] * count
        + [pl.BlockSpec((rows, n), lambda i: (0, 0))] * count,
        out_specs=pl.BlockSpec((bm, n), lambda i: (i, 0)),
        out_shape=jax.ShapeDtypeStruct((m, n), BF16),
        compiler_params=pltpu.CompilerParams(vmem_limit_bytes=40 * MIB),
        cost_estimate=pl.CostEstimate(
            flops=2 * count * rows * m * n,
            bytes_accessed=2 * (count * rows * (m + n) + m * n),
            transcendentals=0,
        ),
    )(*lefts, *rights)


def place_kernel(index, block_ref, out_ref):
    out_ref[...] = block_ref[...].astype(F32)


def place_first(block, index, shape):
    rows, cols = block.shape
    steps = max(1, rows // 128)
    return pl.pallas_call(
        place_kernel,
        grid_spec=pltpu.PrefetchScalarGridSpec(
            num_scalar_prefetch=1,
            grid=(steps,),
            in_specs=[pl.BlockSpec((rows // steps, cols), lambda i, index: (i, 0))],
            out_specs=pl.BlockSpec((rows // steps, cols), lambda i, index: (index[0] * steps + i, 0)),
        ),
        out_shape=jax.ShapeDtypeStruct(shape, F32),
        compiler_params=pltpu.CompilerParams(vmem_limit_bytes=60 * MIB),
        cost_estimate=pl.CostEstimate(
            flops=0, bytes_accessed=6 * rows * cols, transcendentals=0
        ),
    )(index.astype(jnp.int32).reshape(1), block)


def place_of(axis):
    return lax.axis_index(axis).astype(jnp.uint32)


def tp_place():
    t = place_of("tp")
    return lax.div(t, jnp.uint32(CORES)), lax.rem(t, jnp.uint32(CORES))


def shifted(place, shift, size):
    return lax.rem(place + jnp.uint32(shift + 2 * size), jnp.uint32(size))


def rows_at(source, index, count):
    return lax.dynamic_slice_in_dim(source, index * jnp.uint32(count), count, 0)


def cols_at(source, index, count):
    return lax.dynamic_slice_in_dim(source, index * jnp.uint32(count), count, 1)


def put_rows(target, block, index):
    zero = jnp.uint32(0)
    return lax.dynamic_update_slice(target, block, (index * jnp.uint32(block.shape[0]), zero))


def tp_pairs(size, shift, flip):
    rows = size // CORES
    return [
        (y * CORES + c, (y + shift) % rows * CORES + (c ^ flip))
        for y in range(rows)
        for c in range(CORES)
    ]


def after(value, *before):
    return lax.optimization_barrier((value, before))[0]


def tp_near(values):
    size = lax.axis_size("tp")
    return [values] + [
        lax.ppermute(values, "tp", tp_pairs(size, k, 0)) for k in range(1, size // CORES)
    ]


def tp_cross(near):
    return [(v, lax.ppermute(v, "tp", tp_pairs(lax.axis_size("tp"), 0, 1))) for v in near]


def tp_ordered(blocks):
    rows = len(blocks)
    y, c = tp_place()
    out = []
    for want in range(rows):
        for core in range(CORES):
            picks = [jnp.where(c == core, own, other) for own, other in blocks]
            chosen = picks[0]
            for k in range(1, rows):
                chosen = jnp.where(y == (want + k) % rows, picks[k], chosen)
            out.append(chosen)
    return out


def tp_join(near):
    return jnp.concatenate(tp_ordered(tp_cross(near)), axis=1)


class TpSum:
    def __init__(self, partial_sum):
        self.size = lax.axis_size("tp")
        self.rows = self.size // CORES
        self.width = partial_sum.shape[1] // self.size
        self.y, c = tp_place()

        def side(core):
            blocks = [
                cols_at(partial_sum, jnp.uint32(i * CORES) + core, self.width)
                for i in range(self.rows)
            ]
            return jnp.concatenate(blocks, axis=1)

        self.kept = side(c)
        self.arrived = lax.ppermute(side(jnp.uint32(1) - c), "tp", tp_pairs(self.size, 0, 1))

    def across(self, clock):
        def add(kept, arrived):
            return (kept.astype(F32) + arrived.astype(F32)).astype(BF16)

        self.pair = clock(add, self.kept, self.arrived)
        self.moved = [
            lax.ppermute(
                cols_at(self.pair, shifted(self.y, k, self.rows), self.width),
                "tp",
                tp_pairs(self.size, k, 0),
            )
            for k in range(1, self.rows)
        ]

    def total(self, pair, moved):
        total = cols_at(pair, self.y, self.width).astype(F32)
        for part in moved:
            total = total + part.astype(F32)
        return total


def tp_sum(values):
    size = lax.axis_size("tp")
    pair = values + lax.ppermute(values, "tp", tp_pairs(size, 0, 1))
    total = pair
    for k in range(1, size // CORES):
        total = total + lax.ppermute(pair, "tp", tp_pairs(size, k, 0))
    return total


def ring_order(size):
    across = 2 ** (int(math.log2(size)) // 2)
    down = size // across
    order = [a * across for a in range(down)]
    for i, a in enumerate(reversed(range(down))):
        turn = range(1, across) if i % 2 == 0 else reversed(range(1, across))
        order += [a * across + b for b in turn]
    return order


def ring_table():
    order = ring_order(lax.axis_size("ctx"))
    places = [order.index(i) for i in range(len(order))]
    table = jnp.array(places, jnp.uint32)
    own = lax.dynamic_index_in_dim(table, place_of("ctx"), keepdims=False)
    return order, table, own


def ring_shift(order, shift):
    size = len(order)
    return [(order[i], order[(i + shift) % size]) for i in range(size)]


class Clock:
    def __init__(self):
        self.last = []

    def __call__(self, work, *inputs):
        inputs, _ = lax.optimization_barrier((inputs, self.last))
        out = work(*inputs)
        self.last = jax.tree.leaves(out)
        return out


class Ring:
    def __init__(self, clock, grad, way):
        self.clock, self.grad, self.way = clock, grad, way
        self.order, _, self.place = ring_table()
        self.size = len(self.order)
        self.rows = grad.shape[0] // self.size
        self.step = 0
        self.out = None
        self.send(rows_at(grad, self.place, self.rows))

    def send(self, block):
        self.arrived = lax.ppermute(block, "ctx", ring_shift(self.order, self.way))

    def done(self):
        return self.step == 2 * (self.size - 1)

    def turn(self):
        if self.done():
            return
        self.step += 1
        n = self.size
        index = shifted(self.place, -self.way * self.step % n, n)

        def add(arrived):
            own = rows_at(self.grad, index, self.rows)
            return (arrived.astype(F32) + own.astype(F32)).astype(BF16)

        held = self.clock(add if self.step <= n - 1 else lambda arrived: arrived, self.arrived)
        if not self.done():
            self.send(held)
        if self.step == n - 1:
            self.out = self.clock(lambda block: place_first(block, index, self.grad.shape), held)
        elif self.step >= n:
            self.out = self.clock(
                lambda out, block: put_rows(out, block.astype(F32), index), self.out, held
            )


def grid_of(size):
    across = 2 ** (int(math.log2(size)) // 2)
    return size // across, across


class Grid:
    def __init__(self):
        self.down, self.across = grid_of(lax.axis_size("ctx"))
        me = place_of("ctx")
        self.a, self.b = lax.div(me, jnp.uint32(self.across)), lax.rem(me, jnp.uint32(self.across))

    def send_row(self, values, k):
        n = self.across
        pairs = [(a * n + b, a * n + (b + k) % n) for a in range(self.down) for b in range(n)]
        return lax.ppermute(values, "ctx", pairs)

    def send_column(self, values, k):
        n, m = self.across, self.down
        pairs = [(a * n + b, (a + k) % m * n + b) for a in range(m) for b in range(n)]
        return lax.ppermute(values, "ctx", pairs)


def added(parts):
    total = parts[0].astype(F32)
    for part in parts[1:]:
        total = total + part.astype(F32)
    return total.astype(BF16)


class GridGather(Grid):
    def __init__(self, values):
        super().__init__()
        self.flight = [values] + [self.send_row(values, j) for j in range(1, self.across)]

    def second(self, clock):
        row = clock(lambda *parts: jnp.concatenate(parts, axis=0), *self.flight)
        self.flight = [row] + [self.send_column(row, k) for k in range(1, self.down)]

    def joined(self, clock):
        return clock(lambda *parts: jnp.concatenate(parts, axis=0), *self.flight)


def grid_slots():
    grid = Grid()
    down, across = grid.down, grid.across
    every_a = jnp.array([i // across for i in range(down * across)], jnp.uint32)
    every_b = jnp.array([i % across for i in range(down * across)], jnp.uint32)
    k = lax.rem(grid.a + jnp.uint32(down) - every_a, jnp.full_like(every_a, down))
    j = lax.rem(grid.b + jnp.uint32(across) - every_b, jnp.full_like(every_b, across))
    return (k * jnp.uint32(across) + j).astype(jnp.int32)


class GridScatter(Grid):
    def __init__(self, clock, values):
        super().__init__()
        parts = values.reshape((self.down, self.across) + values.shape[1:])
        kept = clock(lambda v: [v[:, j] for j in range(self.across)], parts)
        self.flight = [kept[0]] + [self.send_row(kept[j], -j) for j in range(1, self.across)]

    def second(self, clock):
        held = clock(lambda *parts: added(parts), *self.flight)
        self.flight = [held[0]] + [self.send_column(held[k], -k) for k in range(1, self.down)]

    def result(self, clock):
        return clock(lambda *parts: added(parts), *self.flight)


class GridSum(Grid):
    def __init__(self, grad):
        super().__init__()
        self.half, self.block = grad.shape[0] // self.across, grad.shape[0] // lax.axis_size("ctx")
        self.shape = grad.shape
        self.flight = [rows_at(grad, self.b, self.half)] + [
            self.send_row(rows_at(grad, shifted(self.b, k, self.across), self.half), k)
            for k in range(1, self.across)
        ]

    def second(self, clock):
        held = clock(lambda *parts: added(parts), *self.flight)
        self.flight = [rows_at(held, self.a, self.block)] + [
            self.send_column(rows_at(held, shifted(self.a, k, self.down), self.block), k)
            for k in range(1, self.down)
        ]

    def third(self, clock):
        held = clock(lambda *parts: added(parts), *self.flight)
        self.flight = [held] + [self.send_column(held, k) for k in range(1, self.down)]

    def fourth(self, clock):
        def joined(*blocks):
            half = jnp.zeros((self.half, self.shape[1]), BF16)
            for k, block in enumerate(blocks):
                half = put_rows(half, block, shifted(self.a, -k, self.down))
            return half

        half = clock(joined, *self.flight)
        self.flight = [half] + [self.send_row(half, k) for k in range(1, self.across)]

    def result(self, clock, dtype=F32):
        def joined(*blocks):
            if self.across == 2:
                first, last = self.b == 0, self.b == 1
                sides = [jnp.where(first, *blocks), jnp.where(last, *blocks)]
                return jnp.concatenate(sides, axis=0).astype(dtype)
            out = jnp.zeros(self.shape, dtype)
            for k, block in enumerate(blocks):
                out = put_rows(out, block.astype(dtype), shifted(self.b, -k, self.across))
            return out

        return clock(joined, *self.flight)


class GridSmallSum(Grid):
    def __init__(self, values):
        super().__init__()
        self.flight = [values] + [self.send_row(values, k) for k in range(1, self.across)]

    def in_order(self, place, size, parts):
        rows = jnp.zeros((size,) + parts[0].shape, F32)
        for k, part in enumerate(parts):
            rows = put_rows(rows, part[None], shifted(place, -k, size))
        return jnp.sum(rows, axis=0)

    def second(self, clock):
        held = clock(lambda *parts: self.in_order(self.b, self.across, parts), *self.flight)
        self.flight = [held] + [self.send_column(held, k) for k in range(1, self.down)]

    def result(self, clock):
        return clock(lambda *parts: self.in_order(self.a, self.down, parts), *self.flight)


def row_stats(values):
    mean = jnp.mean(values, axis=-1, keepdims=True)
    centered = values - mean
    var = jnp.mean(centered * centered, axis=-1, keepdims=True)
    return mean, lax.rsqrt(var + EPS)


def gelu_and_slope(values):
    inner = math.sqrt(2.0 / math.pi)
    square = values * values
    tanh = jnp.tanh(inner * values * (1.0 + 0.044715 * square))
    slope = 0.5 * (1.0 + tanh) + 0.5 * values * (1.0 - tanh * tanh) * inner * (
        1.0 + 3.0 * 0.044715 * square
    )
    return 0.5 * values * (1.0 + tanh), slope


def column_sum(values):
    return jnp.sum(values.astype(F32), axis=0)


def shards(
    tokens,
    lengths,
    teacher,
    out_grad,
    w_query,
    b_query,
    w_keyval,
    b_value,
    w_output,
    b_output,
    w_expand,
    b_expand,
    w_shrink,
    b_shrink,
    gain_first,
    bias_first,
    gain_second,
    bias_second,
):
    seqs, rows, part = tokens.shape
    width = w_query.shape[0]
    head = w_keyval.shape[1] // 2
    every = range(seqs)
    position = lax.axis_index("ctx")
    tp_index = place_of("tp")
    y, core = tp_place()
    core_swap = tp_pairs(lax.axis_size("tp"), 0, 1)
    query_pos = position * rows + jnp.arange(rows, dtype=jnp.int32)
    slots = grid_slots()
    info = [
        jnp.concatenate([jnp.stack([lengths[s], position]).astype(jnp.int32), slots]) for s in every
    ]

    def own_cols(values):
        return cols_at(values, tp_index, part)

    def norm_one(values):
        mean, factor = row_stats(values)
        normed = ((values - mean) * factor * full_gain_first + full_bias_first).astype(BF16)
        return (mean, factor), normed

    def my_half(normed):
        return (dot_nn(normed, my_w_kv) + my_kv_bias).astype(BF16)

    def to_queries(normed):
        return (dot_nn(normed, w_query) + b_query.astype(F32)).astype(BF16)

    def both_halves(mine, other):
        sides = [jnp.where(core == 0, mine, other), jnp.where(core == 0, other, mine)]
        return jnp.concatenate(sides, axis=1)

    def norm_two(s, *blocks):
        heads_all = jnp.concatenate(tp_ordered(pairs_of(blocks)), axis=1)
        mid = inputs[s] + dot_nn(heads_all, w_output_all) + full_b_output
        mean, factor = row_stats(mid)
        normed = ((mid - mean) * factor * full_gain_second + full_bias_second).astype(BF16)
        return mid, (mean, factor), normed

    def expand(normed):
        act, slp = gelu_and_slope(dot_nn(normed, w_expand) + b_expand.astype(F32))
        return act.astype(BF16), slp.astype(BF16)

    def pairs_of(flat):
        return [(flat[i], flat[i + 1]) for i in range(0, len(flat), 2)]

    def crossed(near):
        return [block for pair in tp_cross(near) for block in pair]

    def joined(*blocks):
        return jnp.concatenate(tp_ordered(pairs_of(blocks)), axis=1)

    def finish(s, total, pair, moved):
        final = own_cols(middle[s]) + total(pair, moved) + b_shrink.astype(F32)
        valid = (query_pos < lengths[s]).astype(F32)[:, None]
        weight_out = out_grad[s].astype(F32)
        diff = final - teacher[s].astype(F32)
        value = jnp.sum(valid * (weight_out * final + 0.5 * diff * diff))
        grad = valid * (weight_out + diff)
        return final.astype(BF16), value, grad, grad.astype(BF16)

    def hidden_grad(s, grad):
        return (dot_nt(grad, w_shrink) * slope[s].astype(F32)).astype(BF16)

    kv_bias = jnp.concatenate([jnp.zeros((head,), F32), b_value.astype(F32)])
    my_w_kv = cols_at(w_keyval, core, head)
    my_kv_bias = rows_at(kv_bias, core, head)
    clock = Clock()
    source = clock(lambda t: t, tokens[0])
    near0 = tp_near(source)
    w_output_all = lax.all_gather(w_output, "tp", axis=0, tiled=True)
    vectors = (gain_first, bias_first, gain_second, bias_second, b_output)
    vectors = clock(lambda *v: jnp.stack(v), *vectors)
    vectors = tp_join(tp_near(vectors)).astype(F32)
    full_gain_first, full_bias_first, full_gain_second, full_bias_second, full_b_output = vectors
    own_gain_first, own_gain_second = gain_first.astype(F32), gain_second.astype(F32)
    near1 = tp_near(after(tokens[1], near0))

    def enter(*blocks):
        values = joined(*blocks).astype(F32)
        stats, normed = norm_one(values)
        return values, stats, normed, my_half(normed)

    x0, stats0, first0, mine0 = clock(enter, *crossed(near0))
    kv0 = GridGather(mine0)
    q0 = clock(to_queries, first0)
    cross1 = crossed(after(near1, q0))
    kv0.second(clock)
    x1, stats1, first1, mine1 = clock(enter, *cross1)
    kv1 = GridGather(mine1)
    q1 = clock(to_queries, first1)
    kv1.second(clock)
    inputs, stats_one, first, queries = [x0, x1], [stats0, stats1], [first0, first1], [q0, q1]

    mine = kv0.joined(clock)
    every_kv = [clock(both_halves, mine, lax.ppermute(mine, "tp", core_swap))]
    outs = [clock(lambda q, kv: attend(q, kv, info[0], head), q0, every_kv[0])]
    near0 = tp_near(outs[0][1])
    mine = kv1.joined(clock)
    every_kv.append(clock(both_halves, mine, lax.ppermute(mine, "tp", core_swap)))
    outs.append(clock(lambda q, kv: attend(q, kv, info[1], head), q1, every_kv[1]))
    mixed, attended, lse = zip(*outs)
    near1 = tp_near(attended[1])

    mid0, stats0, sec0 = clock(functools.partial(norm_two, 0), *crossed(after(near0, attended[1])))
    act0, slope0 = clock(expand, sec0)
    part0 = clock(lambda act: dot_nn(act, w_shrink).astype(BF16), act0)
    sum0 = TpSum(part0)
    mid1, stats1, sec1 = clock(functools.partial(norm_two, 1), *crossed(after(near1, sec0)))
    sum0.across(clock)
    act1, slope1 = clock(expand, sec1)
    middle, stats_two, second = [mid0, mid1], [stats0, stats1], [sec0, sec1]
    activated, slope = [act0, act1], [slope0, slope1]
    out0, value0, d_final0, g0 = clock(
        lambda *v: finish(0, sum0.total, *v), sum0.pair, sum0.moved
    )
    near_g0 = tp_near(g0)
    part1 = clock(lambda act: dot_nn(act, w_shrink).astype(BF16), act1)
    sum1 = TpSum(part1)
    sum1.across(clock)
    g0_all = clock(joined, *crossed(after(near_g0, part1)))
    d_hidden0 = clock(lambda g: hidden_grad(0, g), g0_all)
    out1, value1, d_final1, g1 = clock(
        lambda *v: finish(1, sum1.total, *v), sum1.pair, sum1.moved
    )
    near_g1 = tp_near(g1)

    def second_partial(hidden):
        return dot_nt(hidden, w_expand).astype(BF16)

    def d_second(back):
        own = clock(back.total, back.pair, back.moved)
        return own, tp_near(own.astype(BF16))

    def norm_two_back(s, *blocks):
        mean, factor = stats_two[s]
        d_all = joined(*blocks).astype(F32)
        scaled = d_all * full_gain_second
        normed = (middle[s] - mean) * factor
        total = jnp.mean(scaled, axis=-1, keepdims=True)
        cross = jnp.mean(scaled * normed, axis=-1, keepdims=True)
        grad = g_shrink_all[s].astype(F32) + factor * (scaled - total - normed * cross)
        grad = grad.astype(BF16)
        return total, cross, grad, dot_nt(grad, w_output).astype(BF16)

    def norm_two_own(s, d_own, total, cross):
        mean, factor = stats_two[s]
        normed = (own_cols(middle[s]) - mean) * factor
        d_mid = d_final[s] + factor * (d_own * own_gain_second - total - normed * cross)
        sums = (jnp.sum(d_own * normed, axis=0), jnp.sum(d_own, axis=0), column_sum(d_mid.astype(BF16)))
        return d_mid, sums

    def attention_back(s, d_attended):
        return attend_back(queries[s], d_attended, mixed[s], lse[s], every_kv[s], info[s], head)

    def swap_halves(d_keyval):
        sent, kept = cols_at(d_keyval, jnp.uint32(1) - core, head), cols_at(d_keyval, core, head)
        return kept, lax.ppermute(sent, "tp", core_swap)

    def add_halves(kept, moved):
        pair = (kept.astype(F32) + moved.astype(F32)).astype(BF16)
        return pair.reshape(-1, yrows, rows // yrows, head)

    partial0 = clock(second_partial, d_hidden0)
    back0 = TpSum(partial0)
    back0.across(clock)
    g1_all = clock(joined, *crossed(after(near_g1, partial0)))
    output = jnp.stack([out0, out1])
    objective = value0 + value1
    d_final, g_shrink, g_shrink_all = [d_final0, d_final1], [g0, g1], [g0_all, g1_all]
    yrows = lax.axis_size("tp") // CORES

    ring_a = Ring(clock, clock(weight_grad, activated, g_shrink_all), 1)
    d_own0, near0 = d_second(back0)
    d_hidden1 = clock(lambda g: hidden_grad(1, g), g1_all)
    d_hidden = [d_hidden0, d_hidden1]
    ring_b = Ring(clock, clock(weight_grad, second, d_hidden), -1)
    ring_a.turn()
    cross0 = crossed(after(near0, ring_b.grad))
    partial1 = clock(second_partial, d_hidden1)
    back1 = TpSum(partial1)
    total0, cross_sum0, g_output0, d_att0 = clock(functools.partial(norm_two_back, 0), *cross0)
    back1.across(clock)
    ring_b.turn()
    ring_a.turn()
    d_query0, d_keyval0 = clock(functools.partial(attention_back, 0), d_att0)
    halves0 = swap_halves(d_keyval0)
    d_own1, near1 = d_second(back1)
    d_mid0, sums0 = clock(functools.partial(norm_two_own, 0), d_own0, total0, cross_sum0)
    ring_b.turn()
    ring_a.turn()
    pair0 = clock(add_halves, *halves0)
    total1, cross_sum1, g_output1, d_att1 = clock(
        functools.partial(norm_two_back, 1), *crossed(after(near1, pair0))
    )
    grad_output = GridSum(clock(weight_grad, attended, (g_output0, g_output1)))
    ring_b.turn()
    ring_a.turn()
    d_query1, d_keyval1 = clock(functools.partial(attention_back, 1), d_att1)
    halves1 = swap_halves(d_keyval1)
    d_mid1, sums1 = clock(functools.partial(norm_two_own, 1), d_own1, total1, cross_sum1)
    d_middle, d_queries = [d_mid0, d_mid1], [d_query0, d_query1]
    ring_b.turn()
    ring_a.turn()
    grad_output.second(clock)
    grad_query = GridSum(clock(weight_grad, first, d_queries))
    pair1 = clock(add_halves, *halves1)
    pair = clock(lambda *v: jnp.concatenate(v, axis=2), pair0, pair1)

    def split(index):
        return lax.dynamic_index_in_dim(pair, index, 1, keepdims=False)

    kept = split(y)
    moved = [
        lax.ppermute(split(shifted(y, k, yrows)), "tp", tp_pairs(lax.axis_size("tp"), k, 0))
        for k in range(1, yrows)
    ]
    ring_b.turn()
    ring_a.turn()
    partials = [
        clock(lambda d: dot_nt(d, w_query).astype(BF16), d_query) for d_query in d_queries
    ]
    sums = [TpSum(p) for p in partials]
    kv_scatter = GridScatter(clock, clock(lambda *parts: added(parts), kept, *moved))
    grad_output.third(clock)
    ring_b.turn()
    ring_a.turn()
    for part_sum in sums:
        part_sum.across(clock)
    kv_scatter.second(clock)
    grad_query.second(clock)
    ring_b.turn()
    ring_a.turn()
    mine = kv_scatter.result(clock).reshape(seqs, -1, head)
    near = tp_near(mine)
    grad_output.fourth(clock)
    ring_b.turn()
    ring_a.turn()
    grad_query.third(clock)

    def join_kv(*blocks):
        blocks = tp_ordered(pairs_of(blocks))
        halves = [jnp.concatenate(blocks[c::CORES], axis=1) for c in range(CORES)]
        return jnp.concatenate(halves, axis=2)

    d_kv_all = clock(join_kv, *crossed(near))
    d_kv = [d_kv_all[s] for s in every]
    grad_kv = GridSum(clock(weight_grad, [own_cols(f) for f in first], d_kv))
    kv_rows = rows_at(w_keyval, tp_index, part)

    def norm_one_back(s, total, pair, moved):
        mean, factor = stats_one[s]
        d_first = total(pair, moved) + dot_nt(d_kv[s], kv_rows)
        normed = (tokens[s].astype(F32) - mean) * factor
        scaled = d_first * own_gain_first
        return d_first, jnp.stack([jnp.sum(scaled, axis=-1), jnp.sum(scaled * normed, axis=-1)])

    d_firsts, row_sums = zip(
        *[
            clock(functools.partial(norm_one_back, s, sums[s].total), sums[s].pair, sums[s].moved)
            for s in every
        ]
    )
    row_sums = tp_sum(jnp.concatenate(row_sums, axis=0))
    ring_b.turn()
    ring_a.turn()
    grad_w_output = grad_output.result(clock)
    grad_kv.second(clock)
    grad_query.fourth(clock)

    def norm_one_end(s, d_first, row_sums):
        mean, factor = stats_one[s]
        total, cross = row_sums[2 * s][:, None] / width, row_sums[2 * s + 1][:, None] / width
        normed = (tokens[s].astype(F32) - mean) * factor
        grad = d_middle[s] + factor * (d_first * own_gain_first - total - normed * cross)
        return grad, (jnp.sum(d_first * normed, axis=0), jnp.sum(d_first, axis=0))

    tokens_grad, sums_first = zip(
        *[clock(functools.partial(norm_one_end, s), d_firsts[s], row_sums) for s in every]
    )
    shares = tp_ordered(tp_cross(tp_near(jnp.broadcast_to(objective, (8, 128)))))
    ring_b.turn()
    ring_a.turn()
    grad_kv.third(clock)
    objective = sum(part_sum[0, 0] for part_sum in shares)
    small = [
        sum(column_sum(d) for d in d_queries),
        sum(column_sum(d[:, head:]) for d in d_kv),
        sums0[2] + sums1[2],
        sum(column_sum(d) for d in d_hidden),
        sum(column_sum(g) for g in g_shrink),
        sums_first[0][0] + sums_first[1][0],
        sums_first[0][1] + sums_first[1][1],
        sums0[0] + sums1[0],
        sums0[1] + sums1[1],
        jnp.broadcast_to(objective, (128,)),
    ]
    small_sum = GridSmallSum(clock(lambda v: jnp.concatenate(v), small))
    grad_w_query = grad_query.result(clock)
    ring_b.turn()
    ring_a.turn()
    grad_kv.fourth(clock)
    small_sum.second(clock)
    ring_b.turn()
    ring_a.turn()
    grad_w_keyval = grad_kv.result(clock, BF16)
    grad_w_keyval = lax.all_gather(grad_w_keyval, "tp", axis=0, tiled=True)
    summed = small_sum.result(clock)
    while not (ring_a.done() and ring_b.done()):
        ring_b.turn()
        ring_a.turn()
    grad_w_keyval = clock(lambda g: g.astype(F32), grad_w_keyval)
    grad_w_shrink, grad_w_expand = ring_a.out, ring_b.out

    pieces, start = [], 0
    for vector in small:
        pieces.append(summed[start : start + vector.shape[0]])
        start += vector.shape[0]
    (
        grad_b_query,
        grad_b_value,
        grad_b_output,
        grad_b_expand,
        grad_b_shrink,
        grad_gain_first,
        grad_bias_first,
        grad_gain_second,
        grad_bias_second,
        grand_total,
    ) = pieces
    loss = grand_total[0] / (jnp.sum(lengths).astype(F32) * width)
    return (
        output,
        jnp.stack(tokens_grad),
        loss,
        grad_w_query,
        grad_b_query,
        grad_w_keyval,
        grad_b_value,
        grad_w_output,
        grad_b_output,
        grad_w_expand,
        grad_b_expand,
        grad_w_shrink,
        grad_b_shrink,
        grad_gain_first,
        grad_bias_first,
        grad_gain_second,
        grad_bias_second,
    )


def solution(mesh):
    placed = (
        P(None, "ctx", "tp"),
        P(),
        P(None, "ctx", "tp"),
        P(None, "ctx", "tp"),
        P(None, "tp"),
        P("tp"),
        P(),
        P(),
        P("tp", None),
        P("tp"),
        P(None, "tp"),
        P("tp"),
        P("tp", None),
        P("tp"),
        P("tp"),
        P("tp"),
        P("tp"),
        P("tp"),
    )
    return jax.shard_map(
        shards,
        mesh=mesh,
        in_specs=placed,
        out_specs=(
            P(None, "ctx", "tp"),
            P(None, "ctx", "tp"),
            P(),
            P(None, "tp"),
            P("tp"),
            P(),
            P(),
            P("tp", None),
            P("tp"),
            P(None, "tp"),
            P("tp"),
            P("tp", None),
            P("tp"),
            P("tp"),
            P("tp"),
            P("tp"),
            P("tp"),
        ),
        check_vma=False,
    )
```

```python
import functools
import math

import jax
import jax.numpy as jnp
from jax import lax
from jax.experimental import pallas as pl
from jax.experimental.pallas import tpu as pltpu
from jax.sharding import PartitionSpec as P

BLOCK = 256
EPS = 1e-05
NEG = -1e30
LOG2E = math.log2(math.e)
CORES = 2
MIB = 2**20
F32 = jnp.float32
BF16 = jnp.bfloat16


def dot_nn(left, right):
    return lax.dot_general(left, right, (((1,), (0,)), ((), ())), preferred_element_type=F32)


def dot_nt(left, right):
    return lax.dot_general(left, right, (((1,), (1,)), ((), ())), preferred_element_type=F32)


def dot_tn(left, right):
    return lax.dot_general(left, right, (((0,), (0,)), ((), ())), preferred_element_type=F32)


def attend_kernel(heads, head, rows, per, info, q_ref, kv_ref, mix_ref, att_ref, lse_ref, acc, top):
    block = pl.program_id(0)
    length, position = info[0], info[1]
    scale = head**-0.5 * LOG2E
    keys = jnp.minimum((position * pl.num_programs(0) + block + 1) * BLOCK, length)
    chunk = per * rows
    acc[...] = jnp.zeros_like(acc)
    top[...] = jnp.full_like(top, NEG)

    def step(index, masked):
        start = index * chunk
        spots = [pl.multiple_of(info[2 + index * per + i] * rows, rows) for i in range(per)]
        k = jnp.concatenate([kv_ref[pl.ds(spot, rows), :head] for spot in spots], axis=0)
        v = jnp.concatenate([kv_ref[pl.ds(spot, rows), head:] for spot in spots], axis=0)
        wide = jnp.concatenate([v, jnp.ones_like(v)], axis=1)
        for h in range(heads):
            s = dot_nt(q_ref[:, h * head : (h + 1) * head], k) * scale
            if masked:
                col = start + lax.broadcasted_iota(jnp.int32, s.shape, 1)
                s = jnp.where(col < keys, s, NEG)
            old = top[h]
            new = jnp.maximum(old, jnp.max(s, axis=1, keepdims=True))
            p = jnp.exp2(s - new[:, :1])
            top[h] = new
            acc[h] = acc[h] * jnp.exp2(old - new)[:, :1] + dot_nn(p.astype(BF16), wide)

    def body(index, carry):
        step(index, False)
        return carry

    whole = keys // chunk
    lax.fori_loop(0, whole, body, 0)

    @pl.when(keys % chunk != 0)
    def _():
        step(whole, True)

    for h in range(heads):
        cols = slice(h * head, (h + 1) * head)
        total = acc[h][:, head:]
        mixed = acc[h][:, :head] / total
        mix_ref[:, cols] = mixed
        att_ref[:, cols] = mixed.astype(BF16)
        lse_ref[:, cols] = top[h] + jnp.log2(total)


def attend(q, kv, info, head):
    rows, width = q.shape
    full = kv.shape[0]
    heads = width // head
    per = math.gcd(full // rows, max(1, 1024 // rows))
    block = pl.BlockSpec((BLOCK, width), lambda i, info: (i, 0))
    pairs = rows * heads * full
    return pl.pallas_call(
        functools.partial(attend_kernel, heads, head, rows, per),
        grid_spec=pltpu.PrefetchScalarGridSpec(
            num_scalar_prefetch=1,
            grid=(rows // BLOCK,),
            in_specs=[block, pl.BlockSpec((full, 2 * head), lambda i, info: (0, 0))],
            out_specs=[block, block, block],
            scratch_shapes=[
                pltpu.VMEM((heads, BLOCK, 2 * head), F32),
                pltpu.VMEM((heads, BLOCK, head), F32),
            ],
        ),
        out_shape=[
            jax.ShapeDtypeStruct((rows, width), F32),
            jax.ShapeDtypeStruct((rows, width), BF16),
            jax.ShapeDtypeStruct((rows, width), F32),
        ],
        compiler_params=pltpu.CompilerParams(vmem_limit_bytes=40 * MIB),
        cost_estimate=pl.CostEstimate(
            flops=8 * pairs * head, bytes_accessed=4 * MIB, transcendentals=pairs
        ),
    )(info, q, kv)


def attend_back_kernel(
    heads, head, rows, per, info, q_ref, do_ref, mix_ref, lse_ref, kv_ref, dq_ref, dkv_ref, dkv, dq, dlt
):
    block = pl.program_id(0)
    length, position = info[0], info[1]
    blocks = pl.num_programs(0)
    factor = head**-0.5
    scale = factor * LOG2E
    chunk = per * rows
    first = (position * blocks + block) * BLOCK
    keys = jnp.where(first < length, jnp.minimum(first + BLOCK, length), 0)

    @pl.when(block == 0)
    def _():
        dkv[...] = jnp.zeros_like(dkv)

    dq[...] = jnp.zeros_like(dq)
    for h in range(heads):
        cols = slice(h * head, (h + 1) * head)
        delta = jnp.sum(do_ref[:, cols].astype(F32) * mix_ref[:, cols], axis=1, keepdims=True)
        dlt[h] = jnp.broadcast_to(delta, (BLOCK, head))

    def step(index, masked):
        start = index * chunk
        spots = [pl.multiple_of(info[2 + index * per + i] * rows, rows) for i in range(per)]
        k = jnp.concatenate([kv_ref[pl.ds(spot, rows), :head] for spot in spots], axis=0)
        v = jnp.concatenate([kv_ref[pl.ds(spot, rows), head:] for spot in spots], axis=0)
        dk_sum = dv_sum = None
        for h in range(heads):
            cols = slice(h * head, (h + 1) * head)
            q, do = q_ref[:, cols], do_ref[:, cols]
            p = jnp.exp2(dot_nt(q, k) * scale - lse_ref[:, h * head : h * head + 1])
            if masked:
                col = start + lax.broadcasted_iota(jnp.int32, p.shape, 1)
                p = jnp.where(col < keys, p, 0.0)
            ds = (p * (dot_nt(do, v) - dlt[h][:, :1])).astype(BF16)
            dq[h] += dot_nn(ds, k)
            dk, dv = dot_tn(ds, q), dot_tn(p.astype(BF16), do)
            dk_sum, dv_sum = (dk, dv) if h == 0 else (dk_sum + dk, dv_sum + dv)
        for i, spot in enumerate(spots):
            part = slice(i * rows, (i + 1) * rows)
            dkv[pl.ds(spot, rows), :head] += dk_sum[part]
            dkv[pl.ds(spot, rows), head:] += dv_sum[part]

    def body(index, carry):
        step(index, False)
        return carry

    whole = keys // chunk
    lax.fori_loop(0, whole, body, 0)

    @pl.when(keys % chunk != 0)
    def _():
        step(whole, True)

    for h in range(heads):
        dq_ref[:, h * head : (h + 1) * head] = (dq[h] * factor).astype(BF16)

    @pl.when(block == blocks - 1)
    def _():
        dkv_ref[:, :head] = (dkv[:, :head] * factor).astype(BF16)
        dkv_ref[:, head:] = dkv[:, head:].astype(BF16)


def attend_back(q, do, mixed, lse, kv, info, head):
    rows, width = q.shape
    full = kv.shape[0]
    heads = width // head
    per = math.gcd(full // rows, max(1, 1024 // rows))
    block = pl.BlockSpec((BLOCK, width), lambda i, info: (i, 0))
    whole = pl.BlockSpec((full, 2 * head), lambda i, info: (0, 0))
    pairs = rows * heads * full
    return pl.pallas_call(
        functools.partial(attend_back_kernel, heads, head, rows, per),
        grid_spec=pltpu.PrefetchScalarGridSpec(
            num_scalar_prefetch=1,
            grid=(rows // BLOCK,),
            in_specs=[block, block, block, block, whole],
            out_specs=[block, whole],
            scratch_shapes=[
                pltpu.VMEM((full, 2 * head), F32),
                pltpu.VMEM((heads, BLOCK, head), F32),
                pltpu.VMEM((heads, BLOCK, head), F32),
            ],
        ),
        out_shape=[
            jax.ShapeDtypeStruct((rows, width), BF16),
            jax.ShapeDtypeStruct((full, 2 * head), BF16),
        ],
        compiler_params=pltpu.CompilerParams(vmem_limit_bytes=56 * MIB),
        cost_estimate=pl.CostEstimate(
            flops=12 * pairs * head, bytes_accessed=8 * MIB, transcendentals=pairs
        ),
    )(info, q, do, mixed, lse, kv)


def grad_kernel(count, *refs):
    total = dot_tn(refs[0][...], refs[count][...])
    for i in range(1, count):
        total += dot_tn(refs[i][...], refs[count + i][...])
    refs[-1][...] = total.astype(BF16)


def weight_grad(lefts, rights):
    rows, m = lefts[0].shape
    n = rights[0].shape[1]
    bm = min(m, 256)
    count = len(lefts)
    return pl.pallas_call(
        functools.partial(grad_kernel, count),
        grid=(m // bm,),
        in_specs=[pl.BlockSpec((rows, bm), lambda i: (0, i))] * count
        + [pl.BlockSpec((rows, n), lambda i: (0, 0))] * count,
        out_specs=pl.BlockSpec((bm, n), lambda i: (i, 0)),
        out_shape=jax.ShapeDtypeStruct((m, n), BF16),
        compiler_params=pltpu.CompilerParams(vmem_limit_bytes=40 * MIB),
        cost_estimate=pl.CostEstimate(
            flops=2 * count * rows * m * n,
            bytes_accessed=2 * (count * rows * (m + n) + m * n),
            transcendentals=0,
        ),
    )(*lefts, *rights)


def pair_kernel(count, *refs):
    out = refs[-1]
    middle = refs[count].shape[1]
    for start, base in ((0, 0), (middle, 2 * count)):
        total = dot_tn(refs[base][...], refs[base + count][...])
        for i in range(1, count):
            total += dot_tn(refs[base + i][...], refs[base + count + i][...])
        out[:, start : start + middle] = total.astype(BF16)


def pair_grad(lefts, rights, more_lefts, more_rights):
    rows, m = lefts[0].shape
    n = rights[0].shape[1]
    bm = min(m, 256)
    count = len(lefts)
    left = [pl.BlockSpec((rows, bm), lambda i: (0, i))] * count
    right = [pl.BlockSpec((rows, n), lambda i: (0, 0))] * count
    return pl.pallas_call(
        functools.partial(pair_kernel, count),
        grid=(m // bm,),
        in_specs=left + right + left + right,
        out_specs=pl.BlockSpec((bm, 2 * n), lambda i: (i, 0)),
        out_shape=jax.ShapeDtypeStruct((m, 2 * n), BF16),
        compiler_params=pltpu.CompilerParams(vmem_limit_bytes=40 * MIB),
        cost_estimate=pl.CostEstimate(
            flops=4 * count * rows * m * n,
            bytes_accessed=4 * (count * rows * (m + n) + m * n),
            transcendentals=0,
        ),
    )(*lefts, *rights, *more_lefts, *more_rights)


def split_kernel(pair, left, right):
    middle = left.shape[1]
    left[...] = pair[:, :middle].astype(F32)
    right[...] = pair[:, middle:].astype(F32).T


def split_pair(pair):
    rows, cols = pair.shape
    middle = cols // 2
    tile = math.gcd(rows, 256)
    return pl.pallas_call(
        split_kernel,
        grid=(rows // tile,),
        in_specs=[pl.BlockSpec((tile, cols), lambda i: (i, 0))],
        out_specs=[
            pl.BlockSpec((tile, middle), lambda i: (i, 0)),
            pl.BlockSpec((middle, tile), lambda i: (0, i)),
        ],
        out_shape=[
            jax.ShapeDtypeStruct((rows, middle), F32),
            jax.ShapeDtypeStruct((middle, rows), F32),
        ],
        compiler_params=pltpu.CompilerParams(vmem_limit_bytes=40 * MIB),
        cost_estimate=pl.CostEstimate(
            flops=0, bytes_accessed=6 * rows * cols, transcendentals=0
        ),
    )(pair)


def back_kernel(x, w, out):
    out[...] = dot_nt(x[...], w[...]).astype(BF16)


def times_transposed(x, w):
    rows, depth = x.shape
    cols = w.shape[0]
    tile = math.gcd(cols, 512)
    return pl.pallas_call(
        back_kernel,
        grid=(cols // tile,),
        in_specs=[
            pl.BlockSpec((rows, depth), lambda i: (0, 0)),
            pl.BlockSpec((tile, depth), lambda i: (i, 0)),
        ],
        out_specs=pl.BlockSpec((rows, tile), lambda i: (0, i)),
        out_shape=jax.ShapeDtypeStruct((rows, cols), BF16),
        compiler_params=pltpu.CompilerParams(vmem_limit_bytes=40 * MIB),
        cost_estimate=pl.CostEstimate(flops=1, bytes_accessed=1, transcendentals=0),
    )(x, w)


def place_kernel(index, block_ref, out_ref):
    out_ref[...] = block_ref[...].astype(F32)


def place_first(block, index, shape):
    rows, cols = block.shape
    steps = max(1, rows // 128)
    return pl.pallas_call(
        place_kernel,
        grid_spec=pltpu.PrefetchScalarGridSpec(
            num_scalar_prefetch=1,
            grid=(steps,),
            in_specs=[pl.BlockSpec((rows // steps, cols), lambda i, index: (i, 0))],
            out_specs=pl.BlockSpec((rows // steps, cols), lambda i, index: (index[0] * steps + i, 0)),
        ),
        out_shape=jax.ShapeDtypeStruct(shape, F32),
        compiler_params=pltpu.CompilerParams(vmem_limit_bytes=60 * MIB),
        cost_estimate=pl.CostEstimate(
            flops=0, bytes_accessed=6 * rows * cols, transcendentals=0
        ),
    )(index.astype(jnp.int32).reshape(1), block)


def place_of(axis):
    return lax.axis_index(axis).astype(jnp.uint32)


def tp_place():
    t = place_of("tp")
    return lax.div(t, jnp.uint32(CORES)), lax.rem(t, jnp.uint32(CORES))


def shifted(place, shift, size):
    return lax.rem(place + jnp.uint32(shift + 2 * size), jnp.uint32(size))


def rows_at(source, index, count):
    return lax.dynamic_slice_in_dim(source, index * jnp.uint32(count), count, 0)


def cols_at(source, index, count):
    return lax.dynamic_slice_in_dim(source, index * jnp.uint32(count), count, 1)


def put_rows(target, block, index):
    zero = jnp.uint32(0)
    return lax.dynamic_update_slice(target, block, (index * jnp.uint32(block.shape[0]), zero))


def tp_pairs(size, shift, flip):
    rows = size // CORES
    return [
        (y * CORES + c, (y + shift) % rows * CORES + (c ^ flip))
        for y in range(rows)
        for c in range(CORES)
    ]


def after(value, *before):
    return lax.optimization_barrier((value, before))[0]


def tp_near(values):
    size = lax.axis_size("tp")
    return [values] + [
        lax.ppermute(values, "tp", tp_pairs(size, k, 0)) for k in range(1, size // CORES)
    ]


def tp_cross(near):
    return [(v, lax.ppermute(v, "tp", tp_pairs(lax.axis_size("tp"), 0, 1))) for v in near]


def tp_ordered(blocks):
    rows = len(blocks)
    y, c = tp_place()
    out = []
    for want in range(rows):
        for core in range(CORES):
            picks = [jnp.where(c == core, own, other) for own, other in blocks]
            chosen = picks[0]
            for k in range(1, rows):
                chosen = jnp.where(y == (want + k) % rows, picks[k], chosen)
            out.append(chosen)
    return out


def tp_join(near):
    return jnp.concatenate(tp_ordered(tp_cross(near)), axis=1)


class TpSum:
    def __init__(self, partial_sum):
        self.size = lax.axis_size("tp")
        self.rows = self.size // CORES
        self.width = partial_sum.shape[1] // self.size
        self.y, c = tp_place()

        def side(core):
            blocks = [
                cols_at(partial_sum, jnp.uint32(i * CORES) + core, self.width)
                for i in range(self.rows)
            ]
            return jnp.concatenate(blocks, axis=1)

        self.kept = side(c)
        self.arrived = lax.ppermute(side(jnp.uint32(1) - c), "tp", tp_pairs(self.size, 0, 1))

    def across(self, clock):
        def add(kept, arrived):
            return (kept.astype(F32) + arrived.astype(F32)).astype(BF16)

        self.pair = clock(add, self.kept, self.arrived)
        self.moved = [
            lax.ppermute(
                cols_at(self.pair, shifted(self.y, k, self.rows), self.width),
                "tp",
                tp_pairs(self.size, k, 0),
            )
            for k in range(1, self.rows)
        ]

    def total(self, pair, moved):
        total = cols_at(pair, self.y, self.width).astype(F32)
        for part in moved:
            total = total + part.astype(F32)
        return total


def tp_sum(values):
    size = lax.axis_size("tp")
    pair = values + lax.ppermute(values, "tp", tp_pairs(size, 0, 1))
    total = pair
    for k in range(1, size // CORES):
        total = total + lax.ppermute(pair, "tp", tp_pairs(size, k, 0))
    return total


def ring_order(size):
    across = 2 ** (int(math.log2(size)) // 2)
    down = size // across
    order = [a * across for a in range(down)]
    for i, a in enumerate(reversed(range(down))):
        turn = range(1, across) if i % 2 == 0 else reversed(range(1, across))
        order += [a * across + b for b in turn]
    return order


def ring_table():
    order = ring_order(lax.axis_size("ctx"))
    places = [order.index(i) for i in range(len(order))]
    table = jnp.array(places, jnp.uint32)
    own = lax.dynamic_index_in_dim(table, place_of("ctx"), keepdims=False)
    return order, table, own


def ring_shift(order, shift):
    size = len(order)
    return [(order[i], order[(i + shift) % size]) for i in range(size)]


class Clock:
    def __init__(self):
        self.last = []

    def __call__(self, work, *inputs):
        inputs, _ = lax.optimization_barrier((inputs, self.last))
        out = work(*inputs)
        self.last = jax.tree.leaves(out)
        return out


class TwoWay:
    def __init__(self):
        self.order, _, self.place = ring_table()
        self.size = len(self.order)
        self.reach = self.size // 2
        self.holding, self.kept = False, None

    def send(self, ahead, back):
        if self.holding:
            self.kept = (ahead, back)
            return
        self.arrived = [
            lax.ppermute(block, "ctx", ring_shift(self.order, way))
            for block, way in ((ahead, 1), (back, -1))
        ]


    def release(self, *before):
        self.holding = False
        if self.kept is not None:
            kept, self.kept = after(self.kept, *before), None
            self.send(*kept)


def halves_of(block):
    middle = block.shape[0] // 2
    return block[:middle], block[middle:]


class RingScatter(TwoWay):
    def __init__(self, clock, own):
        super().__init__()
        self.clock, self.own, self.step = clock, own, 0
        ahead, back = clock(lambda: (halves_of(own(self.reach))[0], halves_of(own(-self.reach))[1]))
        self.send(ahead, back)

    def turn(self):
        self.step += 1
        step, reach = self.step, self.reach
        assert step <= reach

        def combine(ahead, back):
            if step == reach:
                total = self.own(0).astype(F32) + ahead.astype(F32) + back.astype(F32)
                return (total.astype(BF16),)
            first, second = self.own(reach - step), self.own(step - reach)
            if step == 1:
                (near, far), (low, high) = halves_of(first), halves_of(second)
                near, high = added([near, ahead]), added([high, back])
                return jnp.concatenate([near, far]), jnp.concatenate([low, high])
            return added([first, ahead]), added([second, back])

        held = self.clock(combine, *self.arrived)
        if step == reach:
            self.result = held[0]
        else:
            self.send(*held)


class RingGather(TwoWay):
    def __init__(self, clock, block, hold=False):
        super().__init__()
        self.clock, self.step, self.holding = clock, 0, hold
        self.send(block, block)

    def turn(self):
        self.step += 1
        step, reach = self.step, self.reach
        assert step <= reach
        held = self.clock(lambda *blocks: blocks, *self.arrived)
        if step == reach:
            return {reach: jnp.concatenate(held)}
        if step == reach - 1:
            self.send(halves_of(held[0])[0], halves_of(held[1])[1])
        else:
            self.send(*held)
        return {-step: held[0], step: held[1]}


def slot_of(ahead, size):
    ahead = ahead % size
    return 2 * ahead if ahead < size // 2 else 2 * (size - ahead) - 1


def join_slots(blocks):
    size = len(blocks)
    by_slot = {slot_of(ahead, size): block for ahead, block in blocks.items()}
    return jnp.concatenate([by_slot[i] for i in range(size)], axis=0)


def ring_slots():
    order, table, own = ring_table()
    size = len(order)
    ahead = lax.rem(table + jnp.uint32(size) - own, jnp.full((size,), size, jnp.uint32))
    slots = jnp.where(ahead < size // 2, 2 * ahead, 2 * (size - ahead) - 1)
    return slots.astype(jnp.int32)


class RingSum:
    def __init__(self, clock, grad, outs, write):
        self.clock, self.outs, self.write = clock, outs, write
        place, size = ring_table()[2], lax.axis_size("ctx")
        rows = grad.shape[0] // size
        self.place, self.size = place, size
        self.scatter = RingScatter(
            clock, lambda i: rows_at(grad, shifted(place, i % size, size), rows)
        )
        self.gather = None

    def done(self):
        return self.gather is not None and self.gather.step == self.gather.reach

    def release(self):
        (self.gather or self.scatter).release(self.clock.last)

    def turn(self, hold=False):
        if self.done():
            return
        (self.gather or self.scatter).holding = hold
        if self.gather is None:
            self.scatter.turn()
            if self.scatter.step < self.scatter.reach:
                return
            self.gather = RingGather(self.clock, self.scatter.result, hold)
            blocks = {0: self.scatter.result}
        else:
            blocks = self.gather.turn()
        for ahead, block in blocks.items():
            index = shifted(self.place, ahead % self.size, self.size)
            self.outs = self.clock(lambda outs, b: self.write(outs, b, index), self.outs, block)


def added(parts):
    total = parts[0].astype(F32)
    for part in parts[1:]:
        total = total + part.astype(F32)
    return total.astype(BF16)


def row_stats(values):
    mean = jnp.mean(values, axis=-1, keepdims=True)
    centered = values - mean
    var = jnp.mean(centered * centered, axis=-1, keepdims=True)
    return mean, lax.rsqrt(var + EPS)


def gelu_and_slope(values):
    inner = math.sqrt(2.0 / math.pi)
    square = values * values
    tanh = jnp.tanh(inner * values * (1.0 + 0.044715 * square))
    slope = 0.5 * (1.0 + tanh) + 0.5 * values * (1.0 - tanh * tanh) * inner * (
        1.0 + 3.0 * 0.044715 * square
    )
    return 0.5 * values * (1.0 + tanh), slope


def column_sum(values):
    return jnp.sum(values.astype(F32), axis=0)


def shards(
    tokens,
    lengths,
    teacher,
    out_grad,
    w_query,
    b_query,
    w_keyval,
    b_value,
    w_output,
    b_output,
    w_expand,
    b_expand,
    w_shrink,
    b_shrink,
    gain_first,
    bias_first,
    gain_second,
    bias_second,
):
    seqs, rows, part = tokens.shape
    width = w_query.shape[0]
    head = w_keyval.shape[1] // 2
    every = range(seqs)
    position = lax.axis_index("ctx")
    tp_index = place_of("tp")
    y, core = tp_place()
    core_swap = tp_pairs(lax.axis_size("tp"), 0, 1)
    query_pos = position * rows + jnp.arange(rows, dtype=jnp.int32)
    slots = ring_slots()
    info = [
        jnp.concatenate([jnp.stack([lengths[s], position]).astype(jnp.int32), slots]) for s in every
    ]

    def own_cols(values):
        return cols_at(values, tp_index, part)

    def norm_one(values):
        mean, factor = row_stats(values)
        normed = ((values - mean) * factor * full_gain_first + full_bias_first).astype(BF16)
        return (mean, factor), normed

    def my_half(normed):
        return (dot_nn(normed, my_w_kv) + my_kv_bias).astype(BF16)

    def to_queries(normed):
        return (dot_nn(normed, w_query) + b_query.astype(F32)).astype(BF16)

    def both_halves(mine, other):
        sides = [jnp.where(core == 0, mine, other), jnp.where(core == 0, other, mine)]
        return jnp.concatenate(sides, axis=1)

    def norm_two(s, *blocks):
        heads_all = jnp.concatenate(tp_ordered(pairs_of(blocks)), axis=1)
        mid = inputs[s] + dot_nn(heads_all, w_output_all) + full_b_output
        mean, factor = row_stats(mid)
        normed = ((mid - mean) * factor * full_gain_second + full_bias_second).astype(BF16)
        return mid, (mean, factor), normed

    def expand(normed):
        act, slp = gelu_and_slope(dot_nn(normed, w_expand) + b_expand.astype(F32))
        return act.astype(BF16), slp.astype(BF16)

    def pairs_of(flat):
        return [(flat[i], flat[i + 1]) for i in range(0, len(flat), 2)]

    def crossed(near):
        return [block for pair in tp_cross(near) for block in pair]

    def joined(*blocks):
        return jnp.concatenate(tp_ordered(pairs_of(blocks)), axis=1)

    def finish(s, total, pair, moved):
        final = own_cols(middle[s]) + total(pair, moved) + b_shrink.astype(F32)
        valid = (query_pos < lengths[s]).astype(F32)[:, None]
        weight_out = out_grad[s].astype(F32)
        diff = final - teacher[s].astype(F32)
        value = jnp.sum(valid * (weight_out * final + 0.5 * diff * diff))
        grad = valid * (weight_out + diff)
        return final.astype(BF16), value, grad, grad.astype(BF16)

    def hidden_grad(s, grad):
        return (dot_nt(grad, w_shrink) * slope[s].astype(F32)).astype(BF16)

    kv_bias = jnp.concatenate([jnp.zeros((head,), F32), b_value.astype(F32)])
    my_w_kv = cols_at(w_keyval, core, head)
    my_kv_bias = rows_at(kv_bias, core, head)
    clock = Clock()
    source = clock(lambda t: t, tokens[0])
    near0 = tp_near(source)
    w_output_all = lax.all_gather(after(w_output, near0), "tp", axis=0, tiled=True)
    vectors = (gain_first, bias_first, gain_second, bias_second, b_output)
    vectors = clock(lambda *v: jnp.stack(v), *vectors)
    vectors = tp_join(tp_near(vectors)).astype(F32)
    full_gain_first, full_bias_first, full_gain_second, full_bias_second, full_b_output = vectors
    own_gain_first, own_gain_second = gain_first.astype(F32), gain_second.astype(F32)
    near1 = tp_near(after(tokens[1], near0))

    def enter(*blocks):
        values = joined(*blocks).astype(F32)
        stats, normed = norm_one(values)
        return values, stats, normed, my_half(normed)

    x0, stats0, first0, mine0 = clock(enter, *crossed(near0))
    kv0 = RingGather(clock, mine0)
    keys0, keys1 = {0: mine0}, {}
    q0 = clock(to_queries, first0)
    keys0.update(kv0.turn())
    cross1 = crossed(after(near1, clock.last))
    x1, stats1, first1, mine1 = clock(enter, *cross1)
    kv1 = RingGather(clock, mine1)
    keys1[0] = mine1
    keys0.update(kv0.turn())
    q1 = clock(to_queries, first1)
    inputs, stats_one, first, queries = [x0, x1], [stats0, stats1], [first0, first1], [q0, q1]
    while kv0.step < kv0.reach:
        keys0.update(kv0.turn())
        keys1.update(kv1.turn())

    mine = clock(join_slots, keys0)
    other = lax.ppermute(mine, "tp", core_swap)
    keys1.update(kv1.turn())
    every_kv = [clock(both_halves, mine, other)]
    outs = [clock(lambda q, kv: attend(q, kv, info[0], head), q0, every_kv[0])]
    near0 = tp_near(outs[0][1])
    while kv1.step < kv1.reach:
        keys1.update(kv1.turn())
    mine = clock(join_slots, keys1)
    every_kv.append(clock(both_halves, mine, lax.ppermute(mine, "tp", core_swap)))
    outs.append(clock(lambda q, kv: attend(q, kv, info[1], head), q1, every_kv[1]))
    mixed, attended, lse = zip(*outs)
    near1 = tp_near(attended[1])

    mid0, stats0, sec0 = clock(functools.partial(norm_two, 0), *crossed(after(near0, attended[1])))
    act0, slope0 = clock(expand, sec0)
    part0 = clock(lambda act: dot_nn(act, w_shrink).astype(BF16), act0)
    sum0 = TpSum(part0)
    mid1, stats1, sec1 = clock(functools.partial(norm_two, 1), *crossed(after(near1, sec0)))
    sum0.across(clock)
    act1, slope1 = clock(expand, sec1)
    middle, stats_two, second = [mid0, mid1], [stats0, stats1], [sec0, sec1]
    activated, slope = [act0, act1], [slope0, slope1]
    out0, value0, d_final0, g0 = clock(
        lambda *v: finish(0, sum0.total, *v), sum0.pair, sum0.moved
    )
    near_g0 = tp_near(g0)
    part1 = clock(lambda act: dot_nn(act, w_shrink).astype(BF16), act1)
    sum1 = TpSum(part1)
    sum1.across(clock)
    g0_all = clock(joined, *crossed(after(near_g0, part1)))
    d_hidden0 = clock(lambda g: hidden_grad(0, g), g0_all)
    out1, value1, d_final1, g1 = clock(
        lambda *v: finish(1, sum1.total, *v), sum1.pair, sum1.moved
    )
    near_g1 = tp_near(g1)

    def second_partial(hidden):
        return dot_nt(hidden, w_expand).astype(BF16)

    def d_second(back):
        own = clock(back.total, back.pair, back.moved)
        return own, tp_near(own.astype(BF16))

    def norm_two_back(s, *blocks):
        mean, factor = stats_two[s]
        d_all = joined(*blocks).astype(F32)
        scaled = d_all * full_gain_second
        normed = (middle[s] - mean) * factor
        total = jnp.mean(scaled, axis=-1, keepdims=True)
        cross = jnp.mean(scaled * normed, axis=-1, keepdims=True)
        grad = g_shrink_all[s].astype(F32) + factor * (scaled - total - normed * cross)
        grad = grad.astype(BF16)
        return total, cross, grad, dot_nt(grad, w_output).astype(BF16)

    def norm_two_own(s, d_own, total, cross):
        mean, factor = stats_two[s]
        normed = (own_cols(middle[s]) - mean) * factor
        d_mid = d_final[s] + factor * (d_own * own_gain_second - total - normed * cross)
        sums = (jnp.sum(d_own * normed, axis=0), jnp.sum(d_own, axis=0), column_sum(d_mid.astype(BF16)))
        return d_mid, sums

    def attention_back(s, d_attended):
        return attend_back(queries[s], d_attended, mixed[s], lse[s], every_kv[s], info[s], head)

    def swap_halves(d_keyval):
        sent, kept = cols_at(d_keyval, jnp.uint32(1) - core, head), cols_at(d_keyval, core, head)
        return kept, lax.ppermute(sent, "tp", core_swap)

    def add_halves(kept, moved):
        return added([kept, moved]).reshape(-1, yrows, rows // yrows, head)

    back0 = TpSum(clock(times_transposed, d_hidden0, w_expand))
    back0.across(clock)
    g1_all = clock(joined, *crossed(near_g1))
    output = jnp.stack([out0, out1])
    objective = value0 + value1
    d_final, g_shrink, g_shrink_all = [d_final0, d_final1], [g0, g1], [g0_all, g1_all]
    yrows = lax.axis_size("tp") // CORES

    def matrix_sum(grad):
        def write(outs, block, index):
            if outs is None:
                return place_first(block, index, grad.shape)
            return put_rows(outs, block.astype(F32), index)

        return RingSum(clock, grad, None, write)

    ring_s = matrix_sum(clock(weight_grad, activated, g_shrink_all))
    d_own0, near0 = d_second(back0)
    d_hidden1 = clock(lambda g: hidden_grad(1, g), g1_all)
    d_hidden = [d_hidden0, d_hidden1]
    back1 = TpSum(clock(second_partial, d_hidden1))
    ring_s.turn()
    back1.across(clock)
    cross0 = crossed(after(near0, clock.last))
    ring_e = matrix_sum(clock(weight_grad, second, d_hidden))
    total0, cross_sum0, g_output0, d_att0 = clock(functools.partial(norm_two_back, 0), *cross0)
    d_own1, near1 = d_second(back1)
    ring_s.turn()
    d_query0, d_keyval0 = clock(functools.partial(attention_back, 0), d_att0)
    halves0 = swap_halves(d_keyval0)
    ring_e.turn()
    cross1 = crossed(after(near1, clock.last))
    total1, cross_sum1, g_output1, d_att1 = clock(functools.partial(norm_two_back, 1), *cross1)
    ring_s.turn()
    d_query1, d_keyval1 = clock(functools.partial(attention_back, 1), d_att1)
    halves1 = swap_halves(d_keyval1)
    d_queries = [d_query0, d_query1]
    ring_e.turn()
    pair0 = clock(add_halves, *halves0)
    pair1 = clock(add_halves, *halves1)
    pair = clock(lambda *v: jnp.concatenate(v, axis=2), pair0, pair1)

    def split(index):
        return lax.dynamic_index_in_dim(pair, index, 1, keepdims=False)

    kept = split(y)
    moved = [
        lax.ppermute(split(shifted(y, k, yrows)), "tp", tp_pairs(lax.axis_size("tp"), k, 0))
        for k in range(1, yrows)
    ]
    ring_s.turn()
    grad_pair = clock(pair_grad, first, d_queries, (g_output0, g_output1), attended)
    ring_e.turn(hold=True)
    kv_sum = clock(lambda *parts: added(parts), kept, *moved)
    size = lax.axis_size("ctx")
    ring_k = RingScatter(clock, lambda i: kv_sum[slot_of(i, size)])
    partials = [
        clock(lambda d: dot_nt(d, w_query).astype(BF16), d_query) for d_query in d_queries
    ]
    sums = [TpSum(p) for p in partials]
    ring_s.turn(hold=True)
    ring_k.turn()
    for part_sum in sums:
        part_sum.across(clock)
    while ring_k.step < ring_k.reach:
        ring_k.turn()
    near = tp_near(ring_k.result.reshape(seqs, -1, head))
    ring_e.release()
    ring_s.release()
    d_mid0, sums0 = clock(functools.partial(norm_two_own, 0), d_own0, total0, cross_sum0)
    d_mid1, sums1 = clock(functools.partial(norm_two_own, 1), d_own1, total1, cross_sum1)
    d_middle = [d_mid0, d_mid1]
    d_firsts = [clock(part_sum.total, part_sum.pair, part_sum.moved) for part_sum in sums]
    big = [ring_e, ring_s] * size
    big.pop(0).turn()
    big.pop(0).turn()
    shares = clock(
        lambda *v: tp_ordered(pairs_of(v)),
        *crossed(tp_near(jnp.broadcast_to(objective, (8, 128)))),
    )

    def join_kv(*blocks):
        blocks = tp_ordered(pairs_of(blocks))
        halves = [jnp.concatenate(blocks[c::CORES], axis=1) for c in range(CORES)]
        return jnp.concatenate(halves, axis=2)

    d_kv_all = clock(join_kv, *crossed(after(near, clock.last)))
    d_kv = [d_kv_all[s] for s in every]
    grad_kv = clock(weight_grad, [own_cols(f) for f in first], d_kv)
    kv_rows = rows_at(w_keyval, tp_index, part)

    def norm_one_back(s, partial_sum):
        mean, factor = stats_one[s]
        d_first = partial_sum + dot_nt(d_kv[s], kv_rows)
        normed = (tokens[s].astype(F32) - mean) * factor
        scaled = d_first * own_gain_first
        return d_first, jnp.stack([jnp.sum(scaled, axis=-1), jnp.sum(scaled * normed, axis=-1)])

    d_firsts, row_sums = zip(
        *[clock(functools.partial(norm_one_back, s), d_firsts[s]) for s in every]
    )
    row_sums = clock(lambda *v: jnp.concatenate(v, axis=0), *row_sums)
    pair = clock(jnp.add, row_sums, lax.ppermute(row_sums, "tp", core_swap))
    moved = [
        lax.ppermute(pair, "tp", tp_pairs(lax.axis_size("tp"), k, 0)) for k in range(1, yrows)
    ]
    big.pop(0).turn()
    row_sums = clock(lambda *v: sum(v[1:], v[0]), pair, *moved)

    def norm_one_end(s, d_first, row_sums):
        mean, factor = stats_one[s]
        total, cross = row_sums[2 * s][:, None] / width, row_sums[2 * s + 1][:, None] / width
        normed = (tokens[s].astype(F32) - mean) * factor
        grad = d_middle[s] + factor * (d_first * own_gain_first - total - normed * cross)
        return grad, (jnp.sum(d_first * normed, axis=0), jnp.sum(d_first, axis=0))

    tokens_grad, sums_first = zip(
        *[clock(functools.partial(norm_one_end, s), d_firsts[s], row_sums) for s in every]
    )
    objective = sum(part_sum[0, 0] for part_sum in shares)
    small = [
        sum(column_sum(d) for d in d_queries),
        sum(column_sum(d[:, head:]) for d in d_kv),
        sums0[2] + sums1[2],
        sum(column_sum(d) for d in d_hidden),
        sum(column_sum(g) for g in g_shrink),
        sums_first[0][0] + sums_first[1][0],
        sums_first[0][1] + sums_first[1][1],
        sums0[0] + sums1[0],
        sums0[1] + sums1[1],
    ]
    kv_shape = grad_kv.shape
    pieces, rest = [], objective
    for _ in range(3):
        pieces.append(rest.astype(BF16).astype(F32))
        rest = rest - pieces[-1]
    small.append(jnp.concatenate([jnp.broadcast_to(piece, (128,)) for piece in pieces]))
    count = sum(v.shape[0] for v in small)
    more_rows = -(-count // (32 * kv_shape[1])) * 32

    def pack(kv, vectors):
        vectors = list(vectors) + [jnp.zeros((more_rows * kv_shape[1] - count,), F32)]
        vectors = jnp.concatenate(vectors).astype(BF16).reshape(more_rows, kv_shape[1])
        return jnp.concatenate([kv, vectors], axis=0)

    packed = clock(pack, grad_kv, small)
    big.pop(0).turn()
    big.pop(0).turn()
    ring_g = RingGather(clock, packed)
    every_packed = {0: packed}
    while ring_g.step < ring_g.reach:
        big.pop(0).turn()
        every_packed.update(ring_g.turn())
    while not ring_s.done():
        ring_s.turn()
        ring_e.turn()
    ring_m = RingSum(clock, grad_pair, jnp.zeros(grad_pair.shape, BF16), put_rows)
    ring_e.turn()
    ring_m.turn()
    place = ring_table()[2]

    def total_of(blocks):
        rows = jnp.zeros((size * packed.shape[0], kv_shape[1]), BF16)
        for ahead, block in blocks.items():
            rows = put_rows(rows, block, shifted(place, ahead % size, size))
        return jnp.sum(rows.reshape((size,) + packed.shape).astype(F32), axis=0)

    packed_sum = clock(total_of, every_packed)
    kv_near = tp_near(packed_sum[: kv_shape[0]].astype(BF16))
    while not (ring_m.done() and ring_e.done()):
        ring_e.turn()
        ring_m.turn()
    grad_w_query, grad_w_output = clock(split_pair, ring_m.outs)
    kv_blocks = tp_ordered(tp_cross(kv_near))
    grad_w_keyval = jnp.concatenate(kv_blocks, axis=0).astype(F32)
    summed = packed_sum[kv_shape[0] :].reshape(-1)
    grad_w_shrink, grad_w_expand = ring_s.outs, ring_e.outs

    pieces, start = [], 0
    for vector in small:
        pieces.append(summed[start : start + vector.shape[0]])
        start += vector.shape[0]
    (
        grad_b_query,
        grad_b_value,
        grad_b_output,
        grad_b_expand,
        grad_b_shrink,
        grad_gain_first,
        grad_bias_first,
        grad_gain_second,
        grad_bias_second,
        grand_total,
    ) = pieces
    grand_total = grand_total[0] + grand_total[128] + grand_total[256]
    loss = grand_total / (jnp.sum(lengths).astype(F32) * width)
    return (
        output,
        jnp.stack(tokens_grad),
        loss,
        grad_w_query,
        grad_b_query,
        grad_w_keyval,
        grad_b_value,
        grad_w_output,
        grad_b_output,
        grad_w_expand,
        grad_b_expand,
        grad_w_shrink,
        grad_b_shrink,
        grad_gain_first,
        grad_bias_first,
        grad_gain_second,
        grad_bias_second,
    )


def solution(mesh):
    placed = (
        P(None, "ctx", "tp"),
        P(),
        P(None, "ctx", "tp"),
        P(None, "ctx", "tp"),
        P(None, "tp"),
        P("tp"),
        P(),
        P(),
        P("tp", None),
        P("tp"),
        P(None, "tp"),
        P("tp"),
        P("tp", None),
        P("tp"),
        P("tp"),
        P("tp"),
        P("tp"),
        P("tp"),
    )
    return jax.shard_map(
        shards,
        mesh=mesh,
        in_specs=placed,
        out_specs=(
            P(None, "ctx", "tp"),
            P(None, "ctx", "tp"),
            P(),
            P(None, "tp"),
            P("tp"),
            P(),
            P(),
            P("tp", None),
            P("tp"),
            P(None, "tp"),
            P("tp"),
            P("tp", None),
            P("tp"),
            P("tp"),
            P("tp"),
            P("tp"),
            P("tp"),
        ),
        check_vma=False,
    )
```

```python
import functools
import math

import jax
import jax.numpy as jnp
from jax import lax
from jax.experimental import pallas as pl
from jax.experimental.pallas import tpu as pltpu
from jax.sharding import PartitionSpec as P

BLOCK = 256
EPS = 1e-05
NEG = -1e30
LOG2E = math.log2(math.e)
CORES = 2
MIB = 2**20
F32 = jnp.float32
BF16 = jnp.bfloat16


def dot_nn(left, right):
    return lax.dot_general(left, right, (((1,), (0,)), ((), ())), preferred_element_type=F32)


def dot_nt(left, right):
    return lax.dot_general(left, right, (((1,), (1,)), ((), ())), preferred_element_type=F32)


def dot_tn(left, right):
    return lax.dot_general(left, right, (((0,), (0,)), ((), ())), preferred_element_type=F32)


def attend_kernel(heads, head, rows, per, info, q_ref, kv_ref, mix_ref, att_ref, lse_ref, acc, top):
    block = pl.program_id(0)
    length, position = info[0], info[1]
    scale = head**-0.5 * LOG2E
    keys = jnp.minimum((position * pl.num_programs(0) + block + 1) * BLOCK, length)
    chunk = per * rows
    acc[...] = jnp.zeros_like(acc)
    top[...] = jnp.full_like(top, NEG)

    def step(index, masked):
        start = index * chunk
        spots = [pl.multiple_of(info[2 + index * per + i] * rows, rows) for i in range(per)]
        k = jnp.concatenate([kv_ref[pl.ds(spot, rows), :head] for spot in spots], axis=0)
        v = jnp.concatenate([kv_ref[pl.ds(spot, rows), head:] for spot in spots], axis=0)
        wide = jnp.concatenate([v, jnp.ones_like(v)], axis=1)
        for h in range(heads):
            s = dot_nt(q_ref[:, h * head : (h + 1) * head], k) * scale
            if masked:
                col = start + lax.broadcasted_iota(jnp.int32, s.shape, 1)
                s = jnp.where(col < keys, s, NEG)
            old = top[h]
            new = jnp.maximum(old, jnp.max(s, axis=1, keepdims=True))
            p = jnp.exp2(s - new[:, :1])
            top[h] = new
            acc[h] = acc[h] * jnp.exp2(old - new)[:, :1] + dot_nn(p.astype(BF16), wide)

    def body(index, carry):
        step(index, False)
        return carry

    whole = keys // chunk
    lax.fori_loop(0, whole, body, 0)

    @pl.when(keys % chunk != 0)
    def _():
        step(whole, True)

    for h in range(heads):
        cols = slice(h * head, (h + 1) * head)
        total = acc[h][:, head:]
        mixed = acc[h][:, :head] / total
        mix_ref[:, cols] = mixed
        att_ref[:, cols] = mixed.astype(BF16)
        lse_ref[:, cols] = top[h] + jnp.log2(total)


def attend(q, kv, info, head):
    rows, width = q.shape
    full = kv.shape[0]
    heads = width // head
    per = math.gcd(full // rows, max(1, 1024 // rows))
    block = pl.BlockSpec((BLOCK, width), lambda i, info: (i, 0))
    pairs = rows * heads * full
    return pl.pallas_call(
        functools.partial(attend_kernel, heads, head, rows, per),
        grid_spec=pltpu.PrefetchScalarGridSpec(
            num_scalar_prefetch=1,
            grid=(rows // BLOCK,),
            in_specs=[block, pl.BlockSpec((full, 2 * head), lambda i, info: (0, 0))],
            out_specs=[block, block, block],
            scratch_shapes=[
                pltpu.VMEM((heads, BLOCK, 2 * head), F32),
                pltpu.VMEM((heads, BLOCK, head), F32),
            ],
        ),
        out_shape=[
            jax.ShapeDtypeStruct((rows, width), F32),
            jax.ShapeDtypeStruct((rows, width), BF16),
            jax.ShapeDtypeStruct((rows, width), F32),
        ],
        compiler_params=pltpu.CompilerParams(vmem_limit_bytes=40 * MIB),
        cost_estimate=pl.CostEstimate(
            flops=8 * pairs * head, bytes_accessed=4 * MIB, transcendentals=pairs
        ),
    )(info, q, kv)


def attend_back_kernel(
    heads, head, rows, per, info, q_ref, do_ref, mix_ref, lse_ref, kv_ref, dq_ref, dkv_ref, dkv, dq, dlt
):
    block = pl.program_id(0)
    length, position = info[0], info[1]
    blocks = pl.num_programs(0)
    factor = head**-0.5
    scale = factor * LOG2E
    chunk = per * rows
    first = (position * blocks + block) * BLOCK
    keys = jnp.where(first < length, jnp.minimum(first + BLOCK, length), 0)

    @pl.when(block == 0)
    def _():
        dkv[...] = jnp.zeros_like(dkv)

    dq[...] = jnp.zeros_like(dq)
    for h in range(heads):
        cols = slice(h * head, (h + 1) * head)
        delta = jnp.sum(do_ref[:, cols].astype(F32) * mix_ref[:, cols], axis=1, keepdims=True)
        dlt[h] = jnp.broadcast_to(delta, (BLOCK, head))

    def step(index, masked):
        start = index * chunk
        spots = [pl.multiple_of(info[2 + index * per + i] * rows, rows) for i in range(per)]
        k = jnp.concatenate([kv_ref[pl.ds(spot, rows), :head] for spot in spots], axis=0)
        v = jnp.concatenate([kv_ref[pl.ds(spot, rows), head:] for spot in spots], axis=0)
        dk_sum = dv_sum = None
        for h in range(heads):
            cols = slice(h * head, (h + 1) * head)
            q, do = q_ref[:, cols], do_ref[:, cols]
            p = jnp.exp2(dot_nt(q, k) * scale - lse_ref[:, h * head : h * head + 1])
            if masked:
                col = start + lax.broadcasted_iota(jnp.int32, p.shape, 1)
                p = jnp.where(col < keys, p, 0.0)
            ds = (p * (dot_nt(do, v) - dlt[h][:, :1])).astype(BF16)
            dq[h] += dot_nn(ds, k)
            dk, dv = dot_tn(ds, q), dot_tn(p.astype(BF16), do)
            dk_sum, dv_sum = (dk, dv) if h == 0 else (dk_sum + dk, dv_sum + dv)
        for i, spot in enumerate(spots):
            part = slice(i * rows, (i + 1) * rows)
            dkv[pl.ds(spot, rows), :head] += dk_sum[part]
            dkv[pl.ds(spot, rows), head:] += dv_sum[part]

    def body(index, carry):
        step(index, False)
        return carry

    whole = keys // chunk
    lax.fori_loop(0, whole, body, 0)

    @pl.when(keys % chunk != 0)
    def _():
        step(whole, True)

    for h in range(heads):
        dq_ref[:, h * head : (h + 1) * head] = (dq[h] * factor).astype(BF16)

    @pl.when(block == blocks - 1)
    def _():
        dkv_ref[:, :head] = (dkv[:, :head] * factor).astype(BF16)
        dkv_ref[:, head:] = dkv[:, head:].astype(BF16)


def attend_back(q, do, mixed, lse, kv, info, head):
    rows, width = q.shape
    full = kv.shape[0]
    heads = width // head
    per = math.gcd(full // rows, max(1, 1024 // rows))
    block = pl.BlockSpec((BLOCK, width), lambda i, info: (i, 0))
    whole = pl.BlockSpec((full, 2 * head), lambda i, info: (0, 0))
    pairs = rows * heads * full
    return pl.pallas_call(
        functools.partial(attend_back_kernel, heads, head, rows, per),
        grid_spec=pltpu.PrefetchScalarGridSpec(
            num_scalar_prefetch=1,
            grid=(rows // BLOCK,),
            in_specs=[block, block, block, block, whole],
            out_specs=[block, whole],
            scratch_shapes=[
                pltpu.VMEM((full, 2 * head), F32),
                pltpu.VMEM((heads, BLOCK, head), F32),
                pltpu.VMEM((heads, BLOCK, head), F32),
            ],
        ),
        out_shape=[
            jax.ShapeDtypeStruct((rows, width), BF16),
            jax.ShapeDtypeStruct((full, 2 * head), BF16),
        ],
        compiler_params=pltpu.CompilerParams(vmem_limit_bytes=56 * MIB),
        cost_estimate=pl.CostEstimate(
            flops=12 * pairs * head, bytes_accessed=8 * MIB, transcendentals=pairs
        ),
    )(info, q, do, mixed, lse, kv)


def grad_kernel(count, *refs):
    total = dot_tn(refs[0][...], refs[count][...])
    for i in range(1, count):
        total += dot_tn(refs[i][...], refs[count + i][...])
    refs[-1][...] = total.astype(BF16)


def weight_grad(lefts, rights):
    rows, m = lefts[0].shape
    n = rights[0].shape[1]
    bm = min(m, 256)
    count = len(lefts)
    return pl.pallas_call(
        functools.partial(grad_kernel, count),
        grid=(m // bm,),
        in_specs=[pl.BlockSpec((rows, bm), lambda i: (0, i))] * count
        + [pl.BlockSpec((rows, n), lambda i: (0, 0))] * count,
        out_specs=pl.BlockSpec((bm, n), lambda i: (i, 0)),
        out_shape=jax.ShapeDtypeStruct((m, n), BF16),
        compiler_params=pltpu.CompilerParams(vmem_limit_bytes=40 * MIB),
        cost_estimate=pl.CostEstimate(
            flops=2 * count * rows * m * n,
            bytes_accessed=2 * (count * rows * (m + n) + m * n),
            transcendentals=0,
        ),
    )(*lefts, *rights)


def pair_kernel(count, *refs):
    out = refs[-1]
    middle = refs[count].shape[1]
    for start, base in ((0, 0), (middle, 2 * count)):
        total = dot_tn(refs[base][...], refs[base + count][...])
        for i in range(1, count):
            total += dot_tn(refs[base + i][...], refs[base + count + i][...])
        out[:, start : start + middle] = total.astype(BF16)


def pair_grad(lefts, rights, more_lefts, more_rights):
    rows, m = lefts[0].shape
    n = rights[0].shape[1]
    bm = min(m, 256)
    count = len(lefts)
    left = [pl.BlockSpec((rows, bm), lambda i: (0, i))] * count
    right = [pl.BlockSpec((rows, n), lambda i: (0, 0))] * count
    return pl.pallas_call(
        functools.partial(pair_kernel, count),
        grid=(m // bm,),
        in_specs=left + right + left + right,
        out_specs=pl.BlockSpec((bm, 2 * n), lambda i: (i, 0)),
        out_shape=jax.ShapeDtypeStruct((m, 2 * n), BF16),
        compiler_params=pltpu.CompilerParams(vmem_limit_bytes=40 * MIB),
        cost_estimate=pl.CostEstimate(
            flops=4 * count * rows * m * n,
            bytes_accessed=4 * (count * rows * (m + n) + m * n),
            transcendentals=0,
        ),
    )(*lefts, *rights, *more_lefts, *more_rights)


def split_kernel(pair, left, right):
    middle = left.shape[1]
    left[...] = pair[:, :middle].astype(F32)
    right[...] = pair[:, middle:].astype(F32).T


def split_pair(pair):
    rows, cols = pair.shape
    middle = cols // 2
    tile = math.gcd(rows, 256)
    return pl.pallas_call(
        split_kernel,
        grid=(rows // tile,),
        in_specs=[pl.BlockSpec((tile, cols), lambda i: (i, 0))],
        out_specs=[
            pl.BlockSpec((tile, middle), lambda i: (i, 0)),
            pl.BlockSpec((middle, tile), lambda i: (0, i)),
        ],
        out_shape=[
            jax.ShapeDtypeStruct((rows, middle), F32),
            jax.ShapeDtypeStruct((middle, rows), F32),
        ],
        compiler_params=pltpu.CompilerParams(vmem_limit_bytes=40 * MIB),
        cost_estimate=pl.CostEstimate(
            flops=0, bytes_accessed=6 * rows * cols, transcendentals=0
        ),
    )(pair)


def back_kernel(x, w, out):
    out[...] = dot_nt(x[...], w[...]).astype(BF16)


def times_transposed(x, w):
    rows, depth = x.shape
    cols = w.shape[0]
    tile = math.gcd(cols, 512)
    return pl.pallas_call(
        back_kernel,
        grid=(cols // tile,),
        in_specs=[
            pl.BlockSpec((rows, depth), lambda i: (0, 0)),
            pl.BlockSpec((tile, depth), lambda i: (i, 0)),
        ],
        out_specs=pl.BlockSpec((rows, tile), lambda i: (0, i)),
        out_shape=jax.ShapeDtypeStruct((rows, cols), BF16),
        compiler_params=pltpu.CompilerParams(vmem_limit_bytes=40 * MIB),
        cost_estimate=pl.CostEstimate(flops=1, bytes_accessed=1, transcendentals=0),
    )(x, w)


def place_kernel(index, block_ref, out_ref):
    out_ref[...] = block_ref[...].astype(F32)


def place_first(block, index, shape):
    rows, cols = block.shape
    steps = max(1, rows // 128)
    return pl.pallas_call(
        place_kernel,
        grid_spec=pltpu.PrefetchScalarGridSpec(
            num_scalar_prefetch=1,
            grid=(steps,),
            in_specs=[pl.BlockSpec((rows // steps, cols), lambda i, index: (i, 0))],
            out_specs=pl.BlockSpec((rows // steps, cols), lambda i, index: (index[0] * steps + i, 0)),
        ),
        out_shape=jax.ShapeDtypeStruct(shape, F32),
        compiler_params=pltpu.CompilerParams(vmem_limit_bytes=60 * MIB),
        cost_estimate=pl.CostEstimate(
            flops=0, bytes_accessed=6 * rows * cols, transcendentals=0
        ),
    )(index.astype(jnp.int32).reshape(1), block)


def place_of(axis):
    return lax.axis_index(axis).astype(jnp.uint32)


def tp_place():
    t = place_of("tp")
    return lax.div(t, jnp.uint32(CORES)), lax.rem(t, jnp.uint32(CORES))


def shifted(place, shift, size):
    return lax.rem(place + jnp.uint32(shift + 2 * size), jnp.uint32(size))


def rows_at(source, index, count):
    return lax.dynamic_slice_in_dim(source, index * jnp.uint32(count), count, 0)


def cols_at(source, index, count):
    return lax.dynamic_slice_in_dim(source, index * jnp.uint32(count), count, 1)


def put_rows(target, block, index):
    zero = jnp.uint32(0)
    return lax.dynamic_update_slice(target, block, (index * jnp.uint32(block.shape[0]), zero))


def tp_pairs(size, shift, flip):
    rows = size // CORES
    return [
        (y * CORES + c, (y + shift) % rows * CORES + (c ^ flip))
        for y in range(rows)
        for c in range(CORES)
    ]


def after(value, *before):
    return lax.optimization_barrier((value, before))[0]


def tp_near(values):
    size = lax.axis_size("tp")
    return [values] + [
        lax.ppermute(values, "tp", tp_pairs(size, k, 0)) for k in range(1, size // CORES)
    ]


def tp_cross(near):
    return [(v, lax.ppermute(v, "tp", tp_pairs(lax.axis_size("tp"), 0, 1))) for v in near]


def tp_ordered(blocks):
    rows = len(blocks)
    y, c = tp_place()
    out = []
    for want in range(rows):
        for core in range(CORES):
            picks = [jnp.where(c == core, own, other) for own, other in blocks]
            chosen = picks[0]
            for k in range(1, rows):
                chosen = jnp.where(y == (want + k) % rows, picks[k], chosen)
            out.append(chosen)
    return out


def tp_join(near):
    return jnp.concatenate(tp_ordered(tp_cross(near)), axis=1)


class TpSum:
    def __init__(self, partial_sum):
        self.size = lax.axis_size("tp")
        self.rows = self.size // CORES
        self.width = partial_sum.shape[1] // self.size
        self.y, c = tp_place()

        def side(core):
            blocks = [
                cols_at(partial_sum, jnp.uint32(i * CORES) + core, self.width)
                for i in range(self.rows)
            ]
            return jnp.concatenate(blocks, axis=1)

        self.kept = side(c)
        self.arrived = lax.ppermute(side(jnp.uint32(1) - c), "tp", tp_pairs(self.size, 0, 1))

    def across(self, clock):
        def add(kept, arrived):
            return (kept.astype(F32) + arrived.astype(F32)).astype(BF16)

        self.pair = clock(add, self.kept, self.arrived)
        self.moved = [
            lax.ppermute(
                cols_at(self.pair, shifted(self.y, k, self.rows), self.width),
                "tp",
                tp_pairs(self.size, k, 0),
            )
            for k in range(1, self.rows)
        ]

    def total(self, pair, moved):
        total = cols_at(pair, self.y, self.width).astype(F32)
        for part in moved:
            total = total + part.astype(F32)
        return total


def tp_sum(values):
    size = lax.axis_size("tp")
    pair = values + lax.ppermute(values, "tp", tp_pairs(size, 0, 1))
    total = pair
    for k in range(1, size // CORES):
        total = total + lax.ppermute(pair, "tp", tp_pairs(size, k, 0))
    return total


def ring_order(size):
    across = 2 ** (int(math.log2(size)) // 2)
    down = size // across
    order = [a * across for a in range(down)]
    for i, a in enumerate(reversed(range(down))):
        turn = range(1, across) if i % 2 == 0 else reversed(range(1, across))
        order += [a * across + b for b in turn]
    return order


def ring_table():
    order = ring_order(lax.axis_size("ctx"))
    places = [order.index(i) for i in range(len(order))]
    table = jnp.array(places, jnp.uint32)
    own = lax.dynamic_index_in_dim(table, place_of("ctx"), keepdims=False)
    return order, table, own


def ring_shift(order, shift):
    size = len(order)
    return [(order[i], order[(i + shift) % size]) for i in range(size)]


class Clock:
    def __init__(self):
        self.last = []

    def __call__(self, work, *inputs):
        inputs, _ = lax.optimization_barrier((inputs, self.last))
        out = work(*inputs)
        self.last = jax.tree.leaves(out)
        return out


class TwoWay:
    def __init__(self):
        self.order, _, self.place = ring_table()
        self.size = len(self.order)
        self.reach = self.size // 2
        self.holding, self.kept = False, None

    def send(self, ahead, back):
        if self.holding:
            self.kept = (ahead, back)
            return
        self.arrived = [
            lax.ppermute(block, "ctx", ring_shift(self.order, way))
            for block, way in ((ahead, 1), (back, -1))
        ]


    def release(self, *before):
        self.holding = False
        if self.kept is not None:
            kept, self.kept = after(self.kept, *before), None
            self.send(*kept)


def halves_of(block):
    middle = block.shape[0] // 2
    return block[:middle], block[middle:]


class RingScatter(TwoWay):
    def __init__(self, clock, own):
        super().__init__()
        self.clock, self.own, self.step = clock, own, 0
        ahead, back = clock(lambda: (halves_of(own(self.reach))[0], halves_of(own(-self.reach))[1]))
        self.send(ahead, back)

    def turn(self):
        self.step += 1
        step, reach = self.step, self.reach
        assert step <= reach

        def combine(ahead, back):
            if step == reach:
                total = self.own(0).astype(F32) + ahead.astype(F32) + back.astype(F32)
                return (total.astype(BF16),)
            first, second = self.own(reach - step), self.own(step - reach)
            if step == 1:
                (near, far), (low, high) = halves_of(first), halves_of(second)
                near, high = added([near, ahead]), added([high, back])
                return jnp.concatenate([near, far]), jnp.concatenate([low, high])
            return added([first, ahead]), added([second, back])

        held = self.clock(combine, *self.arrived)
        if step == reach:
            self.result = held[0]
        else:
            self.send(*held)


class RingGather(TwoWay):
    def __init__(self, clock, block, hold=False):
        super().__init__()
        self.clock, self.step, self.holding = clock, 0, hold
        self.send(block, block)

    def turn(self):
        self.step += 1
        step, reach = self.step, self.reach
        assert step <= reach
        held = self.clock(lambda *blocks: blocks, *self.arrived)
        if step == reach:
            return {reach: jnp.concatenate(held)}
        if step == reach - 1:
            self.send(halves_of(held[0])[0], halves_of(held[1])[1])
        else:
            self.send(*held)
        return {-step: held[0], step: held[1]}


def slot_of(ahead, size):
    ahead = ahead % size
    return 2 * ahead if ahead < size // 2 else 2 * (size - ahead) - 1


def join_slots(blocks):
    size = len(blocks)
    by_slot = {slot_of(ahead, size): block for ahead, block in blocks.items()}
    return jnp.concatenate([by_slot[i] for i in range(size)], axis=0)


def ring_slots():
    order, table, own = ring_table()
    size = len(order)
    ahead = lax.rem(table + jnp.uint32(size) - own, jnp.full((size,), size, jnp.uint32))
    slots = jnp.where(ahead < size // 2, 2 * ahead, 2 * (size - ahead) - 1)
    return slots.astype(jnp.int32)


class RingSum:
    def __init__(self, clock, grad, outs, write):
        self.clock, self.outs, self.write = clock, outs, write
        place, size = ring_table()[2], lax.axis_size("ctx")
        rows = grad.shape[0] // size
        self.place, self.size = place, size
        self.scatter = RingScatter(
            clock, lambda i: rows_at(grad, shifted(place, i % size, size), rows)
        )
        self.gather = None

    def done(self):
        return self.gather is not None and self.gather.step == self.gather.reach

    def release(self):
        (self.gather or self.scatter).release(self.clock.last)

    def turn(self, hold=False):
        if self.done():
            return
        (self.gather or self.scatter).holding = hold
        if self.gather is None:
            self.scatter.turn()
            if self.scatter.step < self.scatter.reach:
                return
            self.gather = RingGather(self.clock, self.scatter.result, hold)
            blocks = {0: self.scatter.result}
        else:
            blocks = self.gather.turn()
        for ahead, block in blocks.items():
            index = shifted(self.place, ahead % self.size, self.size)
            self.outs = self.clock(lambda outs, b: self.write(outs, b, index), self.outs, block)


def added(parts):
    total = parts[0].astype(F32)
    for part in parts[1:]:
        total = total + part.astype(F32)
    return total.astype(BF16)


def row_stats(values):
    mean = jnp.mean(values, axis=-1, keepdims=True)
    centered = values - mean
    var = jnp.mean(centered * centered, axis=-1, keepdims=True)
    return mean, lax.rsqrt(var + EPS)


def gelu_and_slope(values):
    inner = math.sqrt(2.0 / math.pi)
    square = values * values
    tanh = jnp.tanh(inner * values * (1.0 + 0.044715 * square))
    slope = 0.5 * (1.0 + tanh) + 0.5 * values * (1.0 - tanh * tanh) * inner * (
        1.0 + 3.0 * 0.044715 * square
    )
    return 0.5 * values * (1.0 + tanh), slope


def column_sum(values):
    return jnp.sum(values.astype(F32), axis=0)


def shards(
    tokens,
    lengths,
    teacher,
    out_grad,
    w_query,
    b_query,
    w_keyval,
    b_value,
    w_output,
    b_output,
    w_expand,
    b_expand,
    w_shrink,
    b_shrink,
    gain_first,
    bias_first,
    gain_second,
    bias_second,
):
    seqs, rows, part = tokens.shape
    width = w_query.shape[0]
    head = w_keyval.shape[1] // 2
    every = range(seqs)
    position = lax.axis_index("ctx")
    tp_index = place_of("tp")
    y, core = tp_place()
    core_swap = tp_pairs(lax.axis_size("tp"), 0, 1)
    query_pos = position * rows + jnp.arange(rows, dtype=jnp.int32)
    slots = ring_slots()
    info = [
        jnp.concatenate([jnp.stack([lengths[s], position]).astype(jnp.int32), slots]) for s in every
    ]

    def own_cols(values):
        return cols_at(values, tp_index, part)

    def norm_one(values):
        mean, factor = row_stats(values)
        normed = ((values - mean) * factor * full_gain_first + full_bias_first).astype(BF16)
        return (mean, factor), normed

    def my_half(normed):
        return (dot_nn(normed, my_w_kv) + my_kv_bias).astype(BF16)

    def to_queries(normed):
        return (dot_nn(normed, w_query) + b_query.astype(F32)).astype(BF16)

    def both_halves(mine, other):
        sides = [jnp.where(core == 0, mine, other), jnp.where(core == 0, other, mine)]
        return jnp.concatenate(sides, axis=1)

    def norm_two(s, *blocks):
        heads_all = jnp.concatenate(tp_ordered(pairs_of(blocks)), axis=1)
        mid = inputs[s] + dot_nn(heads_all, w_output_all) + full_b_output
        mean, factor = row_stats(mid)
        normed = ((mid - mean) * factor * full_gain_second + full_bias_second).astype(BF16)
        return mid, (mean, factor), normed

    def expand(normed):
        act, slp = gelu_and_slope(dot_nn(normed, w_expand) + b_expand.astype(F32))
        return act.astype(BF16), slp.astype(BF16)

    def pairs_of(flat):
        return [(flat[i], flat[i + 1]) for i in range(0, len(flat), 2)]

    def crossed(near):
        return [block for pair in tp_cross(near) for block in pair]

    def joined(*blocks):
        return jnp.concatenate(tp_ordered(pairs_of(blocks)), axis=1)

    def finish(s, total, pair, moved):
        final = own_cols(middle[s]) + total(pair, moved) + b_shrink.astype(F32)
        valid = (query_pos < lengths[s]).astype(F32)[:, None]
        weight_out = out_grad[s].astype(F32)
        diff = final - teacher[s].astype(F32)
        value = jnp.sum(valid * (weight_out * final + 0.5 * diff * diff))
        grad = valid * (weight_out + diff)
        return final.astype(BF16), value, grad, grad.astype(BF16)

    def hidden_grad(s, grad):
        return (dot_nt(grad, w_shrink) * slope[s].astype(F32)).astype(BF16)

    kv_bias = jnp.concatenate([jnp.zeros((head,), F32), b_value.astype(F32)])
    my_w_kv = cols_at(w_keyval, core, head)
    my_kv_bias = rows_at(kv_bias, core, head)
    clock = Clock()
    source = clock(lambda t: t, tokens[0])
    near0 = tp_near(source)
    w_output_all = lax.all_gather(after(w_output, near0), "tp", axis=0, tiled=True)
    vectors = (gain_first, bias_first, gain_second, bias_second, b_output)
    vectors = clock(lambda *v: jnp.stack(v), *vectors)
    vectors = tp_join(tp_near(vectors)).astype(F32)
    full_gain_first, full_bias_first, full_gain_second, full_bias_second, full_b_output = vectors
    own_gain_first, own_gain_second = gain_first.astype(F32), gain_second.astype(F32)
    near1 = tp_near(after(tokens[1], near0))

    def enter(*blocks):
        values = joined(*blocks).astype(F32)
        stats, normed = norm_one(values)
        return values, stats, normed, my_half(normed)

    x0, stats0, first0, mine0 = clock(enter, *crossed(near0))
    kv0 = RingGather(clock, mine0)
    keys0, keys1 = {0: mine0}, {}
    q0 = clock(to_queries, first0)
    keys0.update(kv0.turn())
    cross1 = crossed(after(near1, clock.last))
    x1, stats1, first1, mine1 = clock(enter, *cross1)
    kv1 = RingGather(clock, mine1)
    keys1[0] = mine1
    keys0.update(kv0.turn())
    q1 = clock(to_queries, first1)
    inputs, stats_one, first, queries = [x0, x1], [stats0, stats1], [first0, first1], [q0, q1]
    while kv0.step < kv0.reach:
        keys0.update(kv0.turn())
        keys1.update(kv1.turn())

    mine = clock(join_slots, keys0)
    other = lax.ppermute(mine, "tp", core_swap)
    keys1.update(kv1.turn())
    every_kv = [clock(both_halves, mine, other)]
    outs = [clock(lambda q, kv: attend(q, kv, info[0], head), q0, every_kv[0])]
    near0 = tp_near(outs[0][1])
    while kv1.step < kv1.reach:
        keys1.update(kv1.turn())
    mine = clock(join_slots, keys1)
    every_kv.append(clock(both_halves, mine, lax.ppermute(mine, "tp", core_swap)))
    outs.append(clock(lambda q, kv: attend(q, kv, info[1], head), q1, every_kv[1]))
    mixed, attended, lse = zip(*outs)
    near1 = tp_near(attended[1])

    mid0, stats0, sec0 = clock(functools.partial(norm_two, 0), *crossed(after(near0, attended[1])))
    act0, slope0 = clock(expand, sec0)
    part0 = clock(lambda act: dot_nn(act, w_shrink).astype(BF16), act0)
    sum0 = TpSum(part0)
    mid1, stats1, sec1 = clock(functools.partial(norm_two, 1), *crossed(after(near1, sec0)))
    sum0.across(clock)
    act1, slope1 = clock(expand, sec1)
    middle, stats_two, second = [mid0, mid1], [stats0, stats1], [sec0, sec1]
    activated, slope = [act0, act1], [slope0, slope1]
    out0, value0, d_final0, g0 = clock(
        lambda *v: finish(0, sum0.total, *v), sum0.pair, sum0.moved
    )
    near_g0 = tp_near(g0)
    part1 = clock(lambda act: dot_nn(act, w_shrink).astype(BF16), act1)
    sum1 = TpSum(part1)
    sum1.across(clock)
    g0_all = clock(joined, *crossed(after(near_g0, part1)))
    d_hidden0 = clock(lambda g: hidden_grad(0, g), g0_all)
    out1, value1, d_final1, g1 = clock(
        lambda *v: finish(1, sum1.total, *v), sum1.pair, sum1.moved
    )
    near_g1 = tp_near(g1)

    def second_partial(hidden):
        return dot_nt(hidden, w_expand).astype(BF16)

    def d_second(back):
        own = clock(back.total, back.pair, back.moved)
        return own, tp_near(own.astype(BF16))

    def norm_two_back(s, *blocks):
        mean, factor = stats_two[s]
        d_all = joined(*blocks).astype(F32)
        scaled = d_all * full_gain_second
        normed = (middle[s] - mean) * factor
        total = jnp.mean(scaled, axis=-1, keepdims=True)
        cross = jnp.mean(scaled * normed, axis=-1, keepdims=True)
        grad = g_shrink_all[s].astype(F32) + factor * (scaled - total - normed * cross)
        grad = grad.astype(BF16)
        return total, cross, grad, dot_nt(grad, w_output).astype(BF16)

    def norm_two_own(s, d_own, total, cross):
        mean, factor = stats_two[s]
        normed = (own_cols(middle[s]) - mean) * factor
        d_mid = d_final[s] + factor * (d_own * own_gain_second - total - normed * cross)
        sums = (jnp.sum(d_own * normed, axis=0), jnp.sum(d_own, axis=0), column_sum(d_mid.astype(BF16)))
        return d_mid, sums

    def attention_back(s, d_attended):
        return attend_back(queries[s], d_attended, mixed[s], lse[s], every_kv[s], info[s], head)

    def swap_halves(d_keyval):
        sent, kept = cols_at(d_keyval, jnp.uint32(1) - core, head), cols_at(d_keyval, core, head)
        return kept, lax.ppermute(sent, "tp", core_swap)

    def add_halves(kept, moved):
        return added([kept, moved]).reshape(-1, yrows, rows // yrows, head)

    back0 = TpSum(clock(times_transposed, d_hidden0, w_expand))
    back0.across(clock)
    g1_all = clock(joined, *crossed(near_g1))
    output = jnp.stack([out0, out1])
    objective = value0 + value1
    d_final, g_shrink, g_shrink_all = [d_final0, d_final1], [g0, g1], [g0_all, g1_all]
    yrows = lax.axis_size("tp") // CORES

    def matrix_sum(grad):
        def write(outs, block, index):
            if outs is None:
                return place_first(block, index, grad.shape)
            return put_rows(outs, block.astype(F32), index)

        return RingSum(clock, grad, None, write)

    ring_s = matrix_sum(clock(weight_grad, activated, g_shrink_all))
    d_own0, near0 = d_second(back0)
    d_hidden1 = clock(lambda g: hidden_grad(1, g), g1_all)
    d_hidden = [d_hidden0, d_hidden1]
    back1 = TpSum(clock(second_partial, d_hidden1))
    ring_s.turn()
    back1.across(clock)
    cross0 = crossed(after(near0, clock.last))
    ring_e = matrix_sum(clock(weight_grad, second, d_hidden))
    total0, cross_sum0, g_output0, d_att0 = clock(functools.partial(norm_two_back, 0), *cross0)
    d_own1, near1 = d_second(back1)
    ring_s.turn()
    d_query0, d_keyval0 = clock(functools.partial(attention_back, 0), d_att0)
    halves0 = swap_halves(d_keyval0)
    ring_e.turn()
    cross1 = crossed(after(near1, clock.last))
    total1, cross_sum1, g_output1, d_att1 = clock(functools.partial(norm_two_back, 1), *cross1)
    ring_s.turn()
    d_query1, d_keyval1 = clock(functools.partial(attention_back, 1), d_att1)
    halves1 = swap_halves(d_keyval1)
    d_queries = [d_query0, d_query1]
    ring_e.turn()
    pair0 = clock(add_halves, *halves0)
    pair1 = clock(add_halves, *halves1)
    pair = clock(lambda *v: jnp.concatenate(v, axis=2), pair0, pair1)

    def split(index):
        return lax.dynamic_index_in_dim(pair, index, 1, keepdims=False)

    kept = split(y)
    moved = [
        lax.ppermute(split(shifted(y, k, yrows)), "tp", tp_pairs(lax.axis_size("tp"), k, 0))
        for k in range(1, yrows)
    ]
    ring_s.turn()
    grad_pair = clock(pair_grad, first, d_queries, (g_output0, g_output1), attended)
    ring_e.turn(hold=True)
    kv_sum = clock(lambda *parts: added(parts), kept, *moved)
    size = lax.axis_size("ctx")
    ring_k = RingScatter(clock, lambda i: kv_sum[slot_of(i, size)])
    partials = [
        clock(lambda d: dot_nt(d, w_query).astype(BF16), d_query) for d_query in d_queries
    ]
    sums = [TpSum(p) for p in partials]
    ring_s.turn(hold=True)
    ring_k.turn()
    for part_sum in sums:
        part_sum.across(clock)
    while ring_k.step < ring_k.reach:
        ring_k.turn()
    near = tp_near(ring_k.result.reshape(seqs, -1, head))
    ring_e.release()
    ring_s.release()
    d_mid0, sums0 = clock(functools.partial(norm_two_own, 0), d_own0, total0, cross_sum0)
    d_mid1, sums1 = clock(functools.partial(norm_two_own, 1), d_own1, total1, cross_sum1)
    d_middle = [d_mid0, d_mid1]
    d_firsts = [clock(part_sum.total, part_sum.pair, part_sum.moved) for part_sum in sums]
    big = [ring_e, ring_s] * size
    big.pop(0).turn()
    big.pop(0).turn()
    shares = clock(
        lambda *v: tp_ordered(pairs_of(v)),
        *crossed(tp_near(jnp.broadcast_to(objective, (8, 128)))),
    )

    def join_kv(*blocks):
        blocks = tp_ordered(pairs_of(blocks))
        halves = [jnp.concatenate(blocks[c::CORES], axis=1) for c in range(CORES)]
        return jnp.concatenate(halves, axis=2)

    d_kv_all = clock(join_kv, *crossed(after(near, clock.last)))
    d_kv = [d_kv_all[s] for s in every]
    grad_kv = clock(weight_grad, [own_cols(f) for f in first], d_kv)
    kv_rows = rows_at(w_keyval, tp_index, part)

    def norm_one_back(s, partial_sum):
        mean, factor = stats_one[s]
        d_first = partial_sum + dot_nt(d_kv[s], kv_rows)
        normed = (tokens[s].astype(F32) - mean) * factor
        scaled = d_first * own_gain_first
        return d_first, jnp.stack([jnp.sum(scaled, axis=-1), jnp.sum(scaled * normed, axis=-1)])

    d_firsts, row_sums = zip(
        *[clock(functools.partial(norm_one_back, s), d_firsts[s]) for s in every]
    )
    row_sums = clock(lambda *v: jnp.concatenate(v, axis=0), *row_sums)
    pair = clock(jnp.add, row_sums, lax.ppermute(row_sums, "tp", core_swap))
    moved = [
        lax.ppermute(pair, "tp", tp_pairs(lax.axis_size("tp"), k, 0)) for k in range(1, yrows)
    ]
    big.pop(0).turn()
    row_sums = clock(lambda *v: sum(v[1:], v[0]), pair, *moved)

    def norm_one_end(s, d_first, row_sums):
        mean, factor = stats_one[s]
        total, cross = row_sums[2 * s][:, None] / width, row_sums[2 * s + 1][:, None] / width
        normed = (tokens[s].astype(F32) - mean) * factor
        grad = d_middle[s] + factor * (d_first * own_gain_first - total - normed * cross)
        return grad, (jnp.sum(d_first * normed, axis=0), jnp.sum(d_first, axis=0))

    tokens_grad, sums_first = zip(
        *[clock(functools.partial(norm_one_end, s), d_firsts[s], row_sums) for s in every]
    )
    objective = sum(part_sum[0, 0] for part_sum in shares)
    small = [
        sum(column_sum(d) for d in d_queries),
        sum(column_sum(d[:, head:]) for d in d_kv),
        sums0[2] + sums1[2],
        sum(column_sum(d) for d in d_hidden),
        sum(column_sum(g) for g in g_shrink),
        sums_first[0][0] + sums_first[1][0],
        sums_first[0][1] + sums_first[1][1],
        sums0[0] + sums1[0],
        sums0[1] + sums1[1],
    ]
    kv_shape = grad_kv.shape
    pieces, rest = [], objective
    for _ in range(3):
        pieces.append(rest.astype(BF16).astype(F32))
        rest = rest - pieces[-1]
    small.append(jnp.concatenate([jnp.broadcast_to(piece, (128,)) for piece in pieces]))
    count = sum(v.shape[0] for v in small)
    more_rows = -(-count // (32 * kv_shape[1])) * 32

    def pack(kv, vectors):
        vectors = list(vectors) + [jnp.zeros((more_rows * kv_shape[1] - count,), F32)]
        vectors = jnp.concatenate(vectors).astype(BF16).reshape(more_rows, kv_shape[1])
        return jnp.concatenate([kv, vectors], axis=0)

    packed = clock(pack, grad_kv, small)
    big.pop(0).turn()
    big.pop(0).turn()
    while not (ring_s.done() and ring_e.done()):
        big.pop(0).turn()
    ring_m = RingSum(clock, grad_pair, jnp.zeros(grad_pair.shape, BF16), put_rows)
    ring_g = RingGather(clock, packed)
    every_packed = {0: packed}
    while ring_g.step < ring_g.reach:
        ring_m.turn()
        every_packed.update(ring_g.turn())
    place = ring_table()[2]

    def total_of(blocks):
        rows = jnp.zeros((size * packed.shape[0], kv_shape[1]), BF16)
        for ahead, block in blocks.items():
            rows = put_rows(rows, block, shifted(place, ahead % size, size))
        return jnp.sum(rows.reshape((size,) + packed.shape).astype(F32), axis=0)

    packed_sum = clock(total_of, every_packed)
    kv_near = tp_near(packed_sum[: kv_shape[0]].astype(BF16))
    while not ring_m.done():
        ring_m.turn()
    grad_w_query, grad_w_output = clock(split_pair, ring_m.outs)
    kv_blocks = tp_ordered(tp_cross(kv_near))
    grad_w_keyval = jnp.concatenate(kv_blocks, axis=0).astype(F32)
    summed = packed_sum[kv_shape[0] :].reshape(-1)
    grad_w_shrink, grad_w_expand = ring_s.outs, ring_e.outs

    pieces, start = [], 0
    for vector in small:
        pieces.append(summed[start : start + vector.shape[0]])
        start += vector.shape[0]
    (
        grad_b_query,
        grad_b_value,
        grad_b_output,
        grad_b_expand,
        grad_b_shrink,
        grad_gain_first,
        grad_bias_first,
        grad_gain_second,
        grad_bias_second,
        grand_total,
    ) = pieces
    grand_total = grand_total[0] + grand_total[128] + grand_total[256]
    loss = grand_total / (jnp.sum(lengths).astype(F32) * width)
    return (
        output,
        jnp.stack(tokens_grad),
        loss,
        grad_w_query,
        grad_b_query,
        grad_w_keyval,
        grad_b_value,
        grad_w_output,
        grad_b_output,
        grad_w_expand,
        grad_b_expand,
        grad_w_shrink,
        grad_b_shrink,
        grad_gain_first,
        grad_bias_first,
        grad_gain_second,
        grad_bias_second,
    )


def solution(mesh):
    placed = (
        P(None, "ctx", "tp"),
        P(),
        P(None, "ctx", "tp"),
        P(None, "ctx", "tp"),
        P(None, "tp"),
        P("tp"),
        P(),
        P(),
        P("tp", None),
        P("tp"),
        P(None, "tp"),
        P("tp"),
        P("tp", None),
        P("tp"),
        P("tp"),
        P("tp"),
        P("tp"),
        P("tp"),
    )
    return jax.shard_map(
        shards,
        mesh=mesh,
        in_specs=placed,
        out_specs=(
            P(None, "ctx", "tp"),
            P(None, "ctx", "tp"),
            P(),
            P(None, "tp"),
            P("tp"),
            P(),
            P(),
            P("tp", None),
            P("tp"),
            P(None, "tp"),
            P("tp"),
            P("tp", None),
            P("tp"),
            P("tp"),
            P("tp"),
            P("tp"),
            P("tp"),
        ),
        check_vma=False,
    )
```
